128 devices in a mesh: ia: 8 (over z, x_hi), ja: 16 (over y, x_lo, core).
Axes of the slice: x: 4 (x_hi: 2, x_lo: 2; x = x_hi * 2 + x_lo), y: 4, z: 4, core: 2. Of those that a mesh axis runs over, the one named last changes fastest.
Arguments:
- positions: float32 [3, 196608], P(None, ('ia', 'ja')), may hold values from -6 to 6
- velocities: float32 [3, 196608], P(None, ('ia', 'ja')), may hold values from -6 to 6
- old_acc: float32 [3, 196608], P(None, ('ia', 'ja')), may hold values from -4 to 4
- old_jerk: float32 [3, 196608], P(None, ('ia', 'ja')), may hold values from -4 to 4
- masses: float32 [196608], P(('ia', 'ja')), may hold values from 0.1 to 10
- elapsed: float32 [196608], P(('ia', 'ja')), may hold values from 0 to 0.5
- levels: int32 [196608], P(('ia', 'ja')), may hold values from 0 to 3
- active_index: int32 [128, 512], P(('ia', 'ja')), may hold values from 0 to 1535, as said below
- active_count: int32 [128], P(('ia', 'ja')), may hold values from 1 to 512, as said below
Outputs:
- new_state: float32 [12, 65536], P(None, ('ia', 'ja'))
The draws below stay inside these ranges and needn't reach their ends.
Inputs may be any that keep to these rules, and one draw needn't show every extreme that they name: `active_index`: within a row all 512 entries differ, also in slots that are not live. `active_count`: one owner has exactly 512 active stars and another exactly 1.
All inputs are finite; a program needn't handle non-finite values.
Results may differ from the reference program's by a relative error of at most 0.00002.
Values sent between devices are 32-bit elements; how exact they have to be, the bound alone decides.
A program may use at most 128 MiB of HBM per device.

```python
import math
import jax
import jax.numpy as jnp
from jax import lax

A_CAP = 512
LEVELS = 4
STARS_DEV = 1536
OWNERS = 128
STARS = 196608


def active_pair(key):
    key_count, key_full, key_low, key_score = jax.random.split(key, 4)
    counts = jax.random.randint(key_count, (OWNERS,), 1, A_CAP + 1)
    full_owner = jax.random.randint(key_full, (), 0, OWNERS)
    low_owner = (full_owner + 1 + jax.random.randint(key_low, (), 0, OWNERS - 1)) % OWNERS
    counts = counts.at[full_owner].set(A_CAP).at[low_owner].set(1)
    scores = jax.random.randint(key_score, (OWNERS, STARS_DEV), 0, 1 << 16) * STARS_DEV
    scores = scores + jnp.arange(STARS_DEV, dtype=jnp.int32)[None, :]
    scores = scores.at[0, 0].set(-2).at[0, STARS_DEV - 1].set(-1)
    order = jnp.argsort(scores, axis=1, stable=True)[:, :A_CAP]
    return (order.astype(jnp.int32), counts.astype(jnp.int32))


def draw_active_index(key, part):
    return active_pair(key)[0]


def draw_active_count(key, part):
    return active_pair(key)[1]


def with_ends(values, key, least, largest):
    extent = values.shape
    place = [jax.random.randint(jax.random.fold_in(key, axis), (), 0, extent[axis]) for axis in range(len(extent))]
    values = values.at[tuple(place)].set(least)
    longest = extent.index(max(extent))
    place[longest] = (place[longest] + 1) % extent[longest]
    return values.at[tuple(place)].set(largest)


def steps_of(key, shape, cuts, low, high):
    gain, own = 1.0, jax.random.fold_in(key, 6)
    for dim, shards_of in cuts:
        steps = jnp.exp(jax.random.uniform(jax.random.fold_in(own, dim), (shards_of,), jnp.float32, low / len(cuts), high / len(cuts)))
        gain = gain * jnp.repeat(steps, shape[dim] // shards_of).reshape([-1 if axis == dim else 1 for axis in range(len(shape))])
    return gain


def centred(rng, shape, scale, most, cuts=(), kind=jnp.bfloat16):
    values = scale * jax.random.normal(rng, shape, jnp.float32)
    if cuts:
        values = values * steps_of(rng, shape, cuts, -0.22, 0.18)
    return jnp.clip(values, -most, most).astype(kind)


def setup_inputs(seed: int = 0) -> dict:
    key_of = jax.random.split(jax.random.key(seed), 10)
    return {
        "positions": centred(key_of[0], (3, STARS), 1.0, 6.0, ((1, 128),), jnp.float32),
        "velocities": centred(key_of[1], (3, STARS), 1.0, 6.0, ((1, 128),), jnp.float32),
        "old_acc": centred(key_of[2], (3, STARS), 0.5, 4.0, ((1, 128),), jnp.float32),
        "old_jerk": centred(key_of[3], (3, STARS), 0.5, 4.0, ((1, 128),), jnp.float32),
        "masses": jnp.clip(jnp.exp(math.log(10.0) - 4.6051702 * jax.random.uniform(key_of[4], (STARS,), jnp.float32) ** steps_of(key_of[4], (STARS,), ((0, 128),), -0.2, 0.2)), 0.1, 10.0),
        "elapsed": jnp.clip(0.5 * jax.random.uniform(key_of[5], (STARS,), jnp.float32) ** steps_of(key_of[5], (STARS,), ((0, 128),), -0.2, 0.2), 0.0, 0.5),
        "levels": with_ends(jax.random.randint(key_of[6], (STARS,), 0, LEVELS), jax.random.fold_in(key_of[6], 1), 0, LEVELS - 1).astype(jnp.int32),
        "active_index": draw_active_index(jax.random.fold_in(key_of[9], 71), 0),
        "active_count": draw_active_count(jax.random.fold_in(key_of[9], 71), 0),
    }


soften = 0.01
step_max = 0.5

def predict(positions, velocities, old_acc, old_jerk, interval):
    tau_sq = 0.5 * interval * interval
    tau_cube = interval * interval * interval / 6.0
    pred_pos = positions + interval * velocities + tau_sq * old_acc + tau_cube * old_jerk
    pred_vel = velocities + interval * old_acc + tau_sq * old_jerk
    return (pred_pos, pred_vel)

def pair_sums(sources, targets):
    gap_x = sources[0][:, None] - targets[0][None, :]
    gap_y = sources[1][:, None] - targets[1][None, :]
    gap_z = sources[2][:, None] - targets[2][None, :]
    drift_x = sources[3][:, None] - targets[3][None, :]
    drift_y = sources[4][:, None] - targets[4][None, :]
    drift_z = sources[5][:, None] - targets[5][None, :]
    dist_sq = gap_x * gap_x + gap_y * gap_y + gap_z * gap_z + soften
    inverse = lax.rsqrt(dist_sq)
    weighted = inverse * inverse * inverse * sources[6][:, None]
    radial = 3.0 * (gap_x * drift_x + gap_y * drift_y + gap_z * drift_z) / dist_sq
    return jnp.stack([lax.optimization_barrier(jnp.sum(gap_x * weighted, axis=0)), lax.optimization_barrier(jnp.sum(gap_y * weighted, axis=0)), lax.optimization_barrier(jnp.sum(gap_z * weighted, axis=0)), lax.optimization_barrier(jnp.sum((drift_x - radial * gap_x) * weighted, axis=0)), lax.optimization_barrier(jnp.sum((drift_y - radial * gap_y) * weighted, axis=0)), lax.optimization_barrier(jnp.sum((drift_z - radial * gap_z) * weighted, axis=0))])

def blocked_sums(sources, targets, block_size):
    columns = targets.shape[1]
    if columns > block_size and columns % block_size == 0:
        pieces = targets.reshape(6, columns // block_size, block_size).transpose(1, 0, 2)
        result = lax.map(lambda piece: pair_sums(sources, piece), pieces)
        return result.transpose(1, 0, 2).reshape(6, columns)
    return pair_sums(sources, targets)

def correct(start_pos, start_vel, start_acc, start_jerk, new_acc, new_jerk, step):
    new_vel = start_vel + (start_acc + new_acc) * step / 2.0 + (start_jerk - new_jerk) * step * step / 12.0
    new_pos = start_pos + (start_vel + new_vel) * step / 2.0 + (start_acc - new_acc) * step * step / 12.0
    return (new_pos, new_vel)

def reference(positions, velocities, old_acc, old_jerk, masses, elapsed, levels, active_index, active_count):
    owners = active_index.shape[0]
    stars_dev = masses.shape[0] // owners
    global_index = (active_index + jnp.arange(owners, dtype=jnp.int32)[:, None] * stars_dev).reshape(-1).astype(jnp.int32)
    live = (jnp.arange(active_index.shape[1], dtype=jnp.int32)[None, :] < active_count[:, None]).reshape(-1)
    level_step = step_max * jnp.exp2(-levels.astype(jnp.float32))
    chosen = jnp.zeros(masses.shape, jnp.float32).at[global_index].max(live.astype(jnp.float32))
    interval = jnp.where(chosen > 0.5, level_step, elapsed)
    pred_pos, pred_vel = predict(positions, velocities, old_acc, old_jerk, interval)
    sources = jnp.concatenate([pred_pos, pred_vel, masses[None, :]], axis=0)
    targets = jnp.take(jnp.concatenate([pred_pos, pred_vel], axis=0), global_index, axis=1)
    sums = blocked_sums(sources, targets, 128) * (1.0 / masses.shape[0])
    new_acc = sums[0:3]
    new_jerk = sums[3:6]
    step = jnp.take(level_step, global_index)[None, :]
    new_pos, new_vel = correct(jnp.take(positions, global_index, axis=1), jnp.take(velocities, global_index, axis=1), jnp.take(old_acc, global_index, axis=1), jnp.take(old_jerk, global_index, axis=1), new_acc, new_jerk, step)
    state = jnp.concatenate([new_pos, new_vel, new_acc, new_jerk], axis=0)
    return jnp.where(live[None, :], state, jnp.float32(0.0))
```

```python
import functools

import jax
import jax.numpy as jnp
from jax import lax
from jax.experimental import pallas as pl
from jax.experimental.pallas import tpu as pltpu
from jax.sharding import PartitionSpec as P

MESH = pl.DeviceIdType.MESH
soften = 0.01
f32 = jnp.float32
bf16 = jnp.bfloat16

STARS = 1536
SLOTS = 512
OWNERS = 128
BLOCK = 256
VMEM_LIMIT = 56 * 2**20


def vmem():
    return pl.BlockSpec(memory_space=pltpu.VMEM)


def smem():
    return pl.BlockSpec(memory_space=pltpu.SMEM)


def split3(x):
    a = x.astype(bf16).astype(f32)
    rest = x - a
    b = rest.astype(bf16).astype(f32)
    return a, b, rest - b


def coords():
    ia, ja = lax.axis_index("ia"), lax.axis_index("ja")
    return ia // 2, ia % 2, ja // 4, (ja // 2) % 2, ja % 2


def device(z, xh, y, xl, core):
    return (z * 2 + xh, y * 4 + xl * 2 + core)


def peers():
    z, xh, y, xl, core = coords()
    x = xh * 2 + xl
    across = device(z, xh, y, xl, 1 - core)
    along_x = [device(z, ((x + d) % 4) // 2, y, ((x + d) % 4) % 2, core) for d in (1, 2, 3)]
    along_y = [device(z, xh, (y + d) % 4, xl, core) for d in (1, 2, 3)]
    along_z = [device((z + d) % 4, xh, y, xl, core) for d in (1, 2, 3)]
    return across, along_x, along_y, along_z


def greet():
    across, along_x, along_y, along_z = peers()
    barrier = pltpu.get_barrier_semaphore()
    for peer in [across] + along_x + along_y + along_z:
        pl.semaphore_signal(barrier, inc=1, device_id=peer, device_id_type=MESH)
    return barrier


def predict(d, step):
    tau_sq = 0.5 * step * step
    tau_cube = step * step * step / 6.0
    pos = d[0:3] + step * d[3:6] + tau_sq * d[6:9] + tau_cube * d[9:12]
    vel = d[3:6] + step * d[6:9] + tau_sq * d[9:12]
    return pos, vel


def gather_kernel(
    pos_ref, vel_ref, acc_ref, jerk_ref, mass_ref, elapsed_ref, levels_ref, index_ref, count_ref,
    all_ref, start_ref, src_ref,
    state, send_sem, recv_sem,
):
    barrier = greet()
    z, xh, y, xl, core = coords()
    across, along_x, along_y, along_z = peers()

    state[...] = jnp.zeros_like(state)
    state[0:3] = pos_ref[...]
    state[3:6] = vel_ref[...]
    state[6:9] = acc_ref[...]
    state[9:12] = jerk_ref[...]
    levels = levels_ref[...]
    step = jnp.where(
        levels == 0, 0.5, jnp.where(levels == 1, 0.25, jnp.where(levels == 2, 0.125, 0.0625))
    ).astype(f32)
    state[12:13] = step

    pick = (lax.broadcasted_iota(jnp.int32, (STARS, SLOTS), 0) == index_ref[...]).astype(f32)
    pick = pick.astype(bf16)
    parts = jnp.concatenate(split3(state[...]), axis=0).astype(bf16)
    rows = jnp.dot(parts, pick, preferred_element_type=f32)
    start = (rows[0:16] + rows[16:32]) + rows[32:48]
    start_ref[...] = start
    pred_pos, pred_vel = predict(start, start[12:13])
    counts = jnp.full((2, SLOTS), count_ref[0], jnp.int32).astype(f32)
    all_ref[z, xh, y, xl, core] = jnp.concatenate([pred_pos, pred_vel, counts], axis=0)

    pl.semaphore_wait(barrier, 10)

    def copies(phase, block, targets):
        out = []
        for k, target in enumerate(targets):
            copy = pltpu.make_async_remote_copy(
                src_ref=block, dst_ref=block, send_sem=send_sem.at[phase, k],
                recv_sem=recv_sem.at[phase, k], device_id=target, device_id_type=MESH,
            )
            copy.start()
            out.append(copy)
        return out

    along_x = copies(0, all_ref.at[z, xh, y, xl, core], along_x)

    live = lax.broadcasted_iota(jnp.int32, (8, SLOTS), 1) < count_ref[0]
    live = live.astype(f32).astype(bf16)
    chosen = lax.dot_general(
        live, pick, (((1,), (1,)), ((), ())), preferred_element_type=f32
    )[0:1]
    interval = jnp.where(chosen > 0.5, step, elapsed_ref[...])
    src_pos, src_vel = predict(state[...], interval)
    mass = mass_ref[...]
    src_ref[...] = jnp.concatenate([src_pos, src_vel, mass, jnp.ones_like(mass)], axis=0)

    for c in along_x:
        c.wait_recv()
    along_y = copies(1, all_ref.at[z, :, y, :, core], along_y)
    for c in along_y:
        c.wait_recv()
    along_z = copies(2, all_ref.at[z, :, :, :, core], along_z)
    over = copies(3, all_ref.at[z, :, :, :, core], [across])
    for d in (1, 2, 3):
        along_z[d - 1].wait_recv()
        over += copies(3 + d, all_ref.at[(z - d + 4) % 4, :, :, :, core], [across])
    for c in over:
        c.wait_recv()
    for c in along_x + along_y + along_z + over:
        c.wait_send()


def pair_kernel(all_ref, src_ref, count_ref, out_ref, comp, sums, hq, hr, fw, fb):
    lane = lax.broadcasted_iota(jnp.int32, (8, 128), 1)

    def pack(o, offset):
        shift = offset % 128
        base = pl.multiple_of(offset - shift, 128)
        x = jnp.concatenate([all_ref[o], jnp.zeros((8, 128), f32)], axis=1)
        x = pltpu.roll(x, shift, 1)
        first = pl.ds(base, 128)
        comp[:, first] = jnp.where(lane < shift, comp[:, first], x[:, 0:128])
        comp[:, pl.ds(base + 128, SLOTS)] = x[:, 128:]
        return offset + count_ref[o]

    total = lax.fori_loop(0, OWNERS, pack, jnp.int32(0))

    src = src_ref[...]
    row = lax.broadcasted_iota(jnp.int32, (8, 1), 0)
    centre = jnp.sum(src, axis=1, keepdims=True) * (1.0 / STARS)
    centre = jnp.where(row < 6, jnp.floor(centre * 64.0 + 0.5) * (1.0 / 64.0), 0.0)
    src = src - centre
    mass = src[6:7]
    s_sq = src[0:1] * src[0:1] + src[1:2] * src[1:2] + src[2:3] * src[2:3]
    s_rv = src[0:1] * src[3:4] + src[1:2] * src[4:5] + src[2:3] * src[5:6]
    zero = jnp.zeros_like(s_sq)
    plain = split3(jnp.concatenate([src[0:3] * -2.0, zero, zero, zero, zero, zero], axis=0))
    swapped = split3(jnp.concatenate([-src[3:6], -src[0:3], zero, zero], axis=0))
    unit_q = (row == 6).astype(f32)
    unit_r = (row == 7).astype(f32)
    sq_parts = jnp.concatenate(split3(s_sq) + (zero,) * 5, axis=0)
    rv_parts = jnp.concatenate(split3(s_rv) + (zero,) * 5, axis=0)
    fill = jnp.zeros((72, STARS), f32)
    hq_rows = jnp.concatenate(
        [plain[0] + unit_q, plain[1], plain[0] + unit_q, plain[1], plain[2], plain[0] + unit_q,
         sq_parts, fill], axis=0)
    hr_rows = jnp.concatenate(
        [swapped[0] + unit_r, swapped[1], swapped[0] + unit_r, swapped[1], swapped[2],
         swapped[0] + unit_r, rv_parts, fill], axis=0)
    hq[...] = hq_rows.T.astype(bf16)
    hr[...] = hr_rows.T.astype(bf16)
    weights = jnp.concatenate([src[0:6], zero + 1.0, zero], axis=0) * mass
    pad8 = jnp.zeros((8, STARS), f32)
    fw[...] = jnp.concatenate(split3(weights) + (pad8,), axis=0).astype(bf16)
    weights = jnp.where((row < 3) | (row == 6), weights, 0.0)
    fb[...] = jnp.concatenate(split3(weights) + (pad8,), axis=0).astype(bf16)

    def block(i, carry):
        cols = pl.ds(pl.multiple_of(i * BLOCK, BLOCK), BLOCK)
        t = comp[:, cols] - centre
        t_sq = t[0:1] * t[0:1] + t[1:2] * t[1:2] + t[2:3] * t[2:3] + soften
        t_rv = t[0:1] * t[3:4] + t[1:2] * t[4:5] + t[2:3] * t[5:6]
        p0, p1, p2 = split3(jnp.concatenate([t[0:6], t_sq, t_rv], axis=0))
        ones = jnp.ones((8, BLOCK), f32)
        g = jnp.concatenate(
            [p0, p0, p1, p1, p0, p2, ones, jnp.zeros((72, BLOCK), f32)], axis=0
        ).astype(bf16)
        q = jnp.dot(hq[...], g, preferred_element_type=f32)
        rv = jnp.dot(hr[...], g, preferred_element_type=f32)
        inv = lax.rsqrt(q)
        inv2 = inv * inv
        w = inv2 * inv
        b = w * inv2 * rv
        w_hi = w.astype(bf16)
        b_hi = b.astype(bf16)
        w_lo = (w - w_hi.astype(f32)).astype(bf16)
        b_lo = (b - b_hi.astype(f32)).astype(bf16)
        sw = jnp.dot(fw[...], w_hi, preferred_element_type=f32)
        sb = jnp.dot(fb[...], b_hi, preferred_element_type=f32)
        swl = jnp.dot(fw[0:16], w_lo, preferred_element_type=f32)
        sbl = jnp.dot(fb[0:16], b_lo, preferred_element_type=f32)
        sw = sw[0:8] + (sw[8:16] + (sw[16:24] + (swl[0:8] + swl[8:16])))
        sb = sb[0:8] + (sb[8:16] + (sb[16:24] + (sbl[0:8] + sbl[8:16])))
        rw = sw - t * sw[6:7]
        rb = sb - t * sb[6:7]
        rb = pltpu.roll(rb, 3, 0)
        sums[:, cols] = rw - jnp.where((row >= 3) & (row < 6), 3.0 * rb, 0.0)
        return carry

    lax.fori_loop(0, (total + BLOCK - 1) // BLOCK, block, 0)

    def unpack(o, offset):
        shift = offset % 128
        base = pl.multiple_of(offset - shift, 128)
        x = sums[:, pl.ds(base, SLOTS + 128)]
        x = pltpu.roll(x, (SLOTS + 128) - shift, 1)
        out_ref[o] = x[:, 0:SLOTS]
        return offset + count_ref[o]

    lax.fori_loop(0, OWNERS, unpack, jnp.int32(0))


def reduce_kernel(
    part_ref, start_ref, count_ref, out_ref,
    got_core, got_z, got_y, got_x, sum_z, sum_y, send_sem, recv_sem,
):
    barrier = greet()
    z, xh, y, xl, core = coords()
    across, along_x, along_y, along_z = peers()
    pl.semaphore_wait(barrier, 10)
    sent = []

    def copy(phase, k, src, dst, target):
        c = pltpu.make_async_remote_copy(
            src_ref=src, dst_ref=dst, send_sem=send_sem.at[phase, k],
            recv_sem=recv_sem.at[phase, k], device_id=target, device_id_type=MESH,
        )
        c.start()
        sent.append(c)
        return c

    over = []
    for d in (1, 2, 3, 4):
        zt = (z + d) % 4
        over.append(copy(0, d - 1, part_ref.at[zt, :, :, :, 1 - core], got_core.at[d - 1], across))
    from_z = []
    for d in (1, 2, 3, 4):
        zt = (z + d) % 4
        over[d - 1].wait_recv()
        sum_z[d - 1] = part_ref[zt, :, :, :, core] + got_core[d - 1]
        if d < 4:
            from_z.append(copy(1, d - 1, sum_z.at[d - 1], got_z.at[d - 1], along_z[d - 1]))
    for c in from_z:
        c.wait_recv()
    sum_z[3] = sum_z[3] + (got_z[0] + got_z[1] + got_z[2])
    from_y = []
    for d in (1, 2, 3):
        yt = (y + d) % 4
        from_y.append(copy(2, d - 1, sum_z.at[3, :, yt], got_y.at[d - 1], along_y[d - 1]))
    for c in from_y:
        c.wait_recv()
    sum_y[...] = sum_z[3, :, y] + (got_y[0] + got_y[1] + got_y[2])
    from_x = []
    x = xh * 2 + xl
    for d in (1, 2, 3):
        xt = (x + d) % 4
        from_x.append(copy(3, d - 1, sum_y.at[xt // 2, xt % 2], got_x.at[d - 1], along_x[d - 1]))
    for c in from_x:
        c.wait_recv()
    total = sum_y[xh, xl] + (got_x[0] + got_x[1] + got_x[2])

    total = total * (1.0 / (STARS * OWNERS))
    start = start_ref[...]
    step = start[12:13]
    acc0, jerk0 = start[6:9], start[9:12]
    acc1, jerk1 = total[0:3], total[3:6]
    vel1 = start[3:6] + (acc0 + acc1) * step / 2.0 + (jerk0 - jerk1) * step * step / 12.0
    pos1 = start[0:3] + (start[3:6] + vel1) * step / 2.0 + (acc0 - acc1) * step * step / 12.0
    state = jnp.concatenate([pos1, vel1, acc1, jerk1], axis=0)
    live = lax.broadcasted_iota(jnp.int32, (12, SLOTS), 1) < count_ref[0]
    out_ref[...] = jnp.where(live, state, 0.0)
    for c in sent:
        c.wait_send()


def shards(
    positions, velocities, old_acc, old_jerk, masses, elapsed, levels, active_index, active_count
):
    every, start, src = pl.pallas_call(
        gather_kernel,
        out_shape=(
            jax.ShapeDtypeStruct((4, 2, 4, 2, 2, 8, SLOTS), f32),
            jax.ShapeDtypeStruct((16, SLOTS), f32),
            jax.ShapeDtypeStruct((8, STARS), f32),
        ),
        in_specs=[vmem()] * 8 + [smem()],
        out_specs=(vmem(), vmem(), vmem()),
        scratch_shapes=[
            pltpu.VMEM((16, STARS), f32),
            pltpu.SemaphoreType.DMA((7, 3)),
            pltpu.SemaphoreType.DMA((7, 3)),
        ],
        compiler_params=pltpu.CompilerParams(
            collective_id=0, has_side_effects=True, vmem_limit_bytes=VMEM_LIMIT
        ),
        name="predict_gather",
    )(
        positions, velocities, old_acc, old_jerk, masses.reshape(1, STARS),
        elapsed.reshape(1, STARS), levels.reshape(1, STARS), active_index, active_count,
    )
    every = every.reshape(OWNERS, 8, SLOTS)
    counts = every[:, 6, 0].astype(jnp.int32)
    parts = pl.pallas_call(
        pair_kernel,
        out_shape=jax.ShapeDtypeStruct((OWNERS, 8, SLOTS), f32),
        in_specs=[vmem(), vmem(), smem()],
        out_specs=vmem(),
        scratch_shapes=[
            pltpu.VMEM((8, OWNERS * SLOTS + SLOTS + 128), f32),
            pltpu.VMEM((8, OWNERS * SLOTS + SLOTS + 128), f32),
            pltpu.VMEM((STARS, 128), bf16),
            pltpu.VMEM((STARS, 128), bf16),
            pltpu.VMEM((32, STARS), bf16),
            pltpu.VMEM((32, STARS), bf16),
        ],
        compiler_params=pltpu.CompilerParams(vmem_limit_bytes=VMEM_LIMIT),
        name="pair_sums",
    )(every, src, counts)
    return pl.pallas_call(
        reduce_kernel,
        out_shape=jax.ShapeDtypeStruct((12, SLOTS), f32),
        in_specs=[vmem(), vmem(), smem()],
        out_specs=vmem(),
        scratch_shapes=[
            pltpu.VMEM((4, 2, 4, 2, 8, SLOTS), f32),
            pltpu.VMEM((3, 2, 4, 2, 8, SLOTS), f32),
            pltpu.VMEM((3, 2, 2, 8, SLOTS), f32),
            pltpu.VMEM((3, 8, SLOTS), f32),
            pltpu.VMEM((4, 2, 4, 2, 8, SLOTS), f32),
            pltpu.VMEM((2, 2, 8, SLOTS), f32),
            pltpu.SemaphoreType.DMA((4, 4)),
            pltpu.SemaphoreType.DMA((4, 4)),
        ],
        compiler_params=pltpu.CompilerParams(
            collective_id=1, has_side_effects=True, vmem_limit_bytes=VMEM_LIMIT
        ),
        name="reduce_correct",
    )(parts.reshape(4, 2, 4, 2, 2, 8, SLOTS), start, active_count)


def solution(mesh):
    every = ("ia", "ja")
    in_specs = (
        P(None, every), P(None, every), P(None, every), P(None, every),
        P(every), P(every), P(every), P(every, None), P(every),
    )
    return jax.shard_map(
        shards, mesh=mesh, in_specs=in_specs, out_specs=P(None, every), check_vma=False
    )
```

```python
import jax
import jax.numpy as jnp
from jax import lax
from jax.experimental import pallas as pl
from jax.experimental.pallas import tpu as pltpu
from jax.sharding import PartitionSpec as P

MESH = pl.DeviceIdType.MESH
soften = 0.01
f32 = jnp.float32
bf16 = jnp.bfloat16
f8 = jnp.float8_e4m3fn

STARS = 1536
SLOTS = 512
OWNERS = 128
BLOCK = 256
CHUNK = 768
ROOM = OWNERS * SLOTS + SLOTS + 128
VMEM_LIMIT = 56 * 2**20
PAIRS = 3
GATHER_ORDER = ("xyz", "yzx", "zxy")
REDUCE_ORDER = (
    ("zyx", (2, 4, 2), (2, 2), lambda r, j: r.at[:, j], lambda r, j: r.at[j // 2, j % 2]),
    ("xzy", (4, 4), (4,), lambda r, j: r.at[j], lambda r, j: r.at[j]),
    ("yxz", (4, 2, 2), (4,), lambda r, j: r.at[:, j // 2, j % 2], lambda r, j: r.at[j]),
)
PLACES = (4, 2, 4, 2, 2, 8, 128)
POS_SCALE = 2.0**-2
VEL_SCALE = 2.0**-8
W_SCALE = 2.0**6


def vmem():
    return pl.BlockSpec(memory_space=pltpu.VMEM)


def smem():
    return pl.BlockSpec(memory_space=pltpu.SMEM)


def split3(x):
    a = x.astype(bf16).astype(f32)
    rest = x - a
    b = rest.astype(bf16).astype(f32)
    return a, b, rest - b


def place():
    ia, ja = lax.axis_index("ia"), lax.axis_index("ja")
    return {"z": ia // 2, "x": (ia % 2) * 2 + (ja // 2) % 2, "y": ja // 4}, ja % 2


def device(at, core):
    return (at["z"] * 2 + at["x"] // 2, at["y"] * 4 + (at["x"] % 2) * 2 + core)


def along(me, core, axis, d):
    return device({**me, axis: (me[axis] + d) % 4}, core)


def view(ref, at, core):
    xh, xl = (slice(None),) * 2 if at["x"] is None else (at["x"] // 2, at["x"] % 2)
    z = slice(None) if at["z"] is None else at["z"]
    y = slice(None) if at["y"] is None else at["y"]
    return ref.at[z, xh, y, xl, core]


def greet():
    me, core = place()
    barrier = pltpu.get_barrier_semaphore()
    peers = [along(me, core, axis, d) for axis in "xyz" for d in (1, 2, 3)]
    for peer in [device(me, 1 - core)] + peers:
        pl.semaphore_signal(barrier, inc=1, device_id=peer, device_id_type=MESH)
    return barrier


def predict(d, step):
    tau_sq = 0.5 * step * step
    tau_cube = step * step * step / 6.0
    pos = d[0:3] + step * d[3:6] + tau_sq * d[6:9] + tau_cube * d[9:12]
    vel = d[3:6] + step * d[6:9] + tau_sq * d[9:12]
    return pos, vel


def flat(ref):
    return jnp.concatenate([ref[i:i + 1, :] for i in range(STARS // 128)], axis=1)


def fold(rows):
    return jnp.concatenate([rows[:, 128 * t:128 * (t + 1)] for t in range(4)], axis=0)


def unfold(blocks):
    return jnp.concatenate(
        [jnp.concatenate([b[2 * t:2 * t + 2] for b in blocks], axis=0) for t in range(4)], axis=1
    )


def gather_kernel(
    pos_ref, vel_ref, acc_ref, jerk_ref, mass_ref, elapsed_ref, levels_ref, index_ref, count_ref,
    all0, all1, all2, start_ref, hq_ref, hr_ref, fw_ref, f8_ref, centre_ref,
    state, send_sem, recv_sem,
):
    every = (all0, all1, all2)
    barrier = greet()
    me, core = place()
    started = []

    def send(p, phase, k, block, target):
        c = pltpu.make_async_remote_copy(
            src_ref=block, dst_ref=block, send_sem=send_sem.at[p, phase, k],
            recv_sem=recv_sem.at[p, phase, k], device_id=target, device_id_type=MESH,
        )
        c.start()
        started.append(c)
        return c

    state[...] = jnp.zeros_like(state)
    state[0:3] = pos_ref[...]
    state[3:6] = vel_ref[...]
    state[6:9] = acc_ref[...]
    state[9:12] = jerk_ref[...]
    levels = flat(levels_ref)
    step = jnp.where(
        levels == 0, 0.5, jnp.where(levels == 1, 0.25, jnp.where(levels == 2, 0.125, 0.0625))
    ).astype(f32)
    state[12:13] = step

    pick = (lax.broadcasted_iota(jnp.int32, (STARS, SLOTS), 0) == index_ref[...]).astype(f32)
    pick = pick.astype(bf16)
    parts = jnp.concatenate(split3(state[...]), axis=0).astype(bf16)
    rows = jnp.dot(parts, pick, preferred_element_type=f32)
    start = (rows[0:16] + rows[16:32]) + rows[32:48]
    start_ref[...] = start
    target = jnp.concatenate(predict(start, start[12:13]), axis=0)
    live = lax.broadcasted_iota(jnp.int32, (8, SLOTS), 1) < count_ref[0]
    view(all0, me, core)[...] = fold(jnp.where(live[0:2], target[0:2], 1e30))
    view(all1, me, core)[...] = fold(target[2:4])
    view(all2, me, core)[...] = fold(target[4:6])

    pl.semaphore_wait(barrier, 10)

    have = [dict(me) for _ in range(PAIRS)]
    flight = [[] for _ in range(PAIRS)]

    def begin(phase):
        for p in range(PAIRS):
            axis = GATHER_ORDER[p][phase]
            flight[p] = [
                send(p, phase, d - 1, view(every[p], have[p], core), along(me, core, axis, d))
                for d in (1, 2, 3)
            ]

    def finish(phase):
        for p in range(PAIRS):
            for c in flight[p]:
                c.wait_recv()
            have[p][GATHER_ORDER[p][phase]] = None

    begin(0)
    chosen = lax.dot_general(
        live.astype(f32).astype(bf16), pick, (((1,), (1,)), ((), ())),
        preferred_element_type=f32,
    )[0:1]
    interval = jnp.where(chosen > 0.5, step, flat(elapsed_ref))
    src = jnp.concatenate(predict(state[...], interval), axis=0)
    finish(0)
    begin(1)

    centre = jnp.sum(src, axis=1, keepdims=True) * (1.0 / STARS)
    centre = jnp.floor(centre * 64.0 + 0.5) * (1.0 / 64.0)
    src = src - centre
    centre = jnp.concatenate([centre, jnp.zeros((2, 1), f32)], axis=0)
    centre_ref[...] = jnp.broadcast_to(centre, (8, 128))
    zero = jnp.zeros((1, STARS), f32)
    weights = jnp.concatenate([src, zero + 1.0, zero], axis=0) * flat(mass_ref)
    pos, vel = src[0:3] * POS_SCALE, src[3:6] * VEL_SCALE
    row = lax.broadcasted_iota(jnp.int32, (8, 1), 0)

    def factors(own, square, unit):
        a, b, c = split3(jnp.concatenate([own, zero, zero], axis=0))
        a = a + (row == unit).astype(f32)
        s = jnp.concatenate(split3(square) + (zero,) * 5, axis=0)
        fill = jnp.zeros((72, STARS), f32)
        return jnp.concatenate([a, b, a, b, c, a, s, fill], axis=0).T.astype(bf16)

    square = pos[0:1] * pos[0:1] + pos[1:2] * pos[1:2] + pos[2:3] * pos[2:3]
    hq_ref[...] = factors(jnp.concatenate([pos * -2.0, zero, zero, zero], axis=0), square, 6)
    finish(1)
    begin(2)
    over = [
        [send(p, 3, 0, view(every[p], have[p], core), device(me, 1 - core))]
        for p in range(PAIRS)
    ]
    product = pos[0:1] * vel[0:1] + pos[1:2] * vel[1:2] + pos[2:3] * vel[2:3]
    hr_ref[...] = factors(jnp.concatenate([-vel, -pos], axis=0), product, 7)
    fill = jnp.zeros((8, STARS), f32)
    fw_ref[...] = jnp.concatenate(split3(weights) + (fill,), axis=0).astype(bf16)
    high = weights.astype(f8).astype(f32)
    f8_ref[...] = jnp.concatenate([high, weights - high, fill, fill], axis=0).astype(f8)

    for d in (1, 2, 3):
        for p in range(PAIRS):
            axis = GATHER_ORDER[p][2]
            flight[p][d - 1].wait_recv()
            came = {**have[p], axis: (me[axis] - d + 4) % 4}
            over[p].append(send(p, 3, d, view(every[p], came, core), device(me, 1 - core)))
    for p in range(PAIRS):
        for c in over[p]:
            c.wait_recv()
    for c in started:
        c.wait_send()


def pair_kernel(
    all0, all1, all2, hq, hr, fw, fl, centre_ref,
    out0, out1, out2,
    comp, sums, factor, raw, counts, count, sem,
):
    outs = (out0, out1, out2)
    marked = jnp.where(all0[...] < 1e29, 0.5, 0.0)
    marked = jnp.sum(marked, axis=1).astype(bf16)
    counted = lax.dot_general(
        jnp.ones((8, 128), bf16), marked, (((1,), (1,)), ((), ())), preferred_element_type=f32
    )
    counts[...] = counted.astype(jnp.int32)
    copy = pltpu.make_async_copy(counts, count, sem)
    copy.start()
    copy.wait()

    lane = lax.broadcasted_iota(jnp.int32, (8, 128), 1)
    blank = jnp.zeros((2, SLOTS), f32)

    def pack(o, offset):
        shift = offset % 128
        base = pl.multiple_of(offset - shift, 128)
        x = jnp.concatenate([unfold((all0[o], all1[o], all2[o])), blank], axis=0)
        x = jnp.concatenate([x, jnp.zeros((8, 128), f32)], axis=1)
        x = pltpu.roll(x, shift, 1)
        first = pl.ds(base, 128)
        comp[:, first] = jnp.where(lane < shift, comp[:, first], x[:, 0:128])
        comp[:, pl.ds(base + 128, SLOTS)] = x[:, 128:]
        return offset + count[0, o]

    total = lax.fori_loop(0, OWNERS, pack, jnp.int32(0))
    blocks = (total + BLOCK - 1) // BLOCK
    centre = centre_ref[:, 0:1]
    row = lax.broadcasted_iota(jnp.int32, (8, 1), 0)
    scale = jnp.where(row < 3, POS_SCALE, VEL_SCALE)

    def columns(i):
        return pl.ds(pl.multiple_of(i * BLOCK, BLOCK), BLOCK)

    def make_factor(i):
        t = (comp[:, columns(i)] - centre) * scale
        square = t[0:1] * t[0:1] + t[1:2] * t[1:2] + t[2:3] * t[2:3] + soften * POS_SCALE**2
        product = t[0:1] * t[3:4] + t[1:2] * t[4:5] + t[2:3] * t[5:6]
        a, b, c = split3(jnp.concatenate([t[0:6], square, product], axis=0))
        ones = jnp.ones((8, BLOCK), f32)
        fill = jnp.zeros((72, BLOCK), f32)
        factor[...] = jnp.concatenate([a, a, b, b, a, c, ones, fill], axis=0).astype(bf16)

    def combine(i):
        sw = raw[0:8] + (raw[8:16] + raw[16:24]) + (raw[64:72] + raw[72:80])
        sb = raw[32:40] + (raw[40:48] + raw[48:56]) + (raw[80:88] + raw[88:96])
        t = comp[:, columns(i)] - centre
        rw = (sw - t * sw[6:7]) * (1.0 / W_SCALE)
        rb = pltpu.roll(sb - t * sb[6:7], 3, 0)
        sums[:, columns(i)] = rw - jnp.where((row >= 3) & (row < 6), 3.0 * rb, 0.0)

    def block(i, carry):
        combine(jnp.maximum(i - 1, 0))
        g = factor[...]
        sw = jnp.zeros((32, BLOCK), f32)
        sb = jnp.zeros((32, BLOCK), f32)
        lw = jnp.zeros((32, BLOCK), f32)
        lb = jnp.zeros((32, BLOCK), f32)
        for first in range(0, STARS, CHUNK):
            part = slice(first, first + CHUNK)
            q = jnp.dot(hq[part], g, preferred_element_type=f32)
            rv = jnp.dot(hr[part], g, preferred_element_type=f32)
            inv = lax.rsqrt(q)
            inv2 = inv * inv
            w = inv2 * inv
            b = w * inv2 * rv
            w_high = w.astype(bf16)
            b_high = b.astype(bf16)
            w_low = (w - w_high.astype(f32)).astype(f8)
            b_low = (b - b_high.astype(f32)).astype(f8)
            sw += jnp.dot(fw[:, part], w_high, preferred_element_type=f32)
            sb += jnp.dot(fw[:, part], b_high, preferred_element_type=f32)
            lw += jnp.dot(fl[:, part], w_low, preferred_element_type=f32)
            lb += jnp.dot(fl[:, part], b_low, preferred_element_type=f32)
        raw[0:32] = sw
        raw[32:64] = sb
        raw[64:80] = lw[0:16]
        raw[80:96] = lb[0:16]
        make_factor(i + 1)
        return carry

    raw[...] = jnp.zeros_like(raw)
    make_factor(0)
    lax.fori_loop(0, blocks, block, 0)
    combine(jnp.maximum(blocks - 1, 0))

    def unpack(o, offset):
        shift = offset % 128
        base = pl.multiple_of(offset - shift, 128)
        x = sums[:, pl.ds(base, SLOTS + 128)]
        x = pltpu.roll(x, (SLOTS + 128) - shift, 1)
        for p in range(PAIRS):
            outs[p][o] = fold(x[2 * p:2 * p + 2, 0:SLOTS])
        return offset + count[0, o]

    lax.fori_loop(0, OWNERS, unpack, jnp.int32(0))


def reduce_kernel(
    part0, part1, part2, start_ref, count_ref, out_ref,
    got_core, got_1, got_2, got_3, sum_1, sum_2, send_sem, recv_sem,
):
    part = (part0, part1, part2)
    barrier = greet()
    me, core = place()
    started = []

    def send(p, phase, k, src, dst, target):
        c = pltpu.make_async_remote_copy(
            src_ref=src, dst_ref=dst, send_sem=send_sem.at[p, phase, k],
            recv_sem=recv_sem.at[p, phase, k], device_id=target, device_id_type=MESH,
        )
        c.start()
        started.append(c)
        return c

    def plane(p, d):
        axis = REDUCE_ORDER[p][0][0]
        return {"x": None, "y": None, "z": None, axis: (me[axis] + d) % 4}

    pl.semaphore_wait(barrier, 10)
    over = [[None] * PAIRS for _ in range(5)]
    for d in (1, 2, 3, 4):
        for p in range(PAIRS):
            over[d][p] = send(
                p, 0, d - 1, view(part[p], plane(p, d), 1 - core), got_core[p].at[d - 1],
                device(me, 1 - core),
            )
    first = [[] for _ in range(PAIRS)]
    for d in (1, 2, 3, 4):
        for p in range(PAIRS):
            over[d][p].wait_recv()
            sum_1[p][d - 1] = view(part[p], plane(p, d), core)[...] + got_core[p][d - 1]
            if d < 4:
                axis = REDUCE_ORDER[p][0][0]
                first[p].append(send(
                    p, 1, d - 1, sum_1[p].at[d - 1], got_1[p].at[d - 1],
                    along(me, core, axis, d),
                ))
    second = [[] for _ in range(PAIRS)]
    for p in range(PAIRS):
        axes, _, _, at2, _ = REDUCE_ORDER[p]
        for c in first[p]:
            c.wait_recv()
        sum_1[p][3] = sum_1[p][3] + (got_1[p][0] + got_1[p][1] + got_1[p][2])
        for d in (1, 2, 3):
            second[p].append(send(
                p, 2, d - 1, at2(sum_1[p].at[3], (me[axes[1]] + d) % 4), got_2[p].at[d - 1],
                along(me, core, axes[1], d),
            ))
    third = [[] for _ in range(PAIRS)]
    for p in range(PAIRS):
        axes, _, _, at2, at3 = REDUCE_ORDER[p]
        for c in second[p]:
            c.wait_recv()
        own = at2(sum_1[p].at[3], me[axes[1]])[...]
        sum_2[p][...] = own + (got_2[p][0] + got_2[p][1] + got_2[p][2])
        for d in (1, 2, 3):
            third[p].append(send(
                p, 3, d - 1, at3(sum_2[p], (me[axes[2]] + d) % 4), got_3[p].at[d - 1],
                along(me, core, axes[2], d),
            ))
    blocks = []
    for p in range(PAIRS):
        axes, _, _, _, at3 = REDUCE_ORDER[p]
        for c in third[p]:
            c.wait_recv()
        own = at3(sum_2[p], me[axes[2]])[...]
        blocks.append(own + (got_3[p][0] + got_3[p][1] + got_3[p][2]))

    total = unfold(blocks) * (1.0 / (STARS * OWNERS))
    start = start_ref[...]
    step = start[12:13]
    acc0, jerk0 = start[6:9], start[9:12]
    acc1, jerk1 = total[0:3], total[3:6]
    vel1 = start[3:6] + (acc0 + acc1) * step / 2.0 + (jerk0 - jerk1) * step * step / 12.0
    pos1 = start[0:3] + (start[3:6] + vel1) * step / 2.0 + (acc0 - acc1) * step * step / 12.0
    state = jnp.concatenate([pos1, vel1, acc1, jerk1], axis=0)
    live = lax.broadcasted_iota(jnp.int32, (12, SLOTS), 1) < count_ref[0]
    out_ref[...] = jnp.where(live, state, 0.0)
    for c in started:
        c.wait_send()


def shards(
    positions, velocities, old_acc, old_jerk, masses, elapsed, levels, active_index, active_count
):
    def lines(a):
        return a.reshape(STARS // 128, 128)

    def params(collective_id=None):
        extra = {} if collective_id is None else {
            "collective_id": collective_id, "has_side_effects": True
        }
        return pltpu.CompilerParams(vmem_limit_bytes=VMEM_LIMIT, **extra)

    *every, start, hq, hr, fw, fl, centre = pl.pallas_call(
        gather_kernel,
        out_shape=[jax.ShapeDtypeStruct(PLACES, f32)] * PAIRS + [
            jax.ShapeDtypeStruct((16, SLOTS), f32),
            jax.ShapeDtypeStruct((STARS, 128), bf16),
            jax.ShapeDtypeStruct((STARS, 128), bf16),
            jax.ShapeDtypeStruct((32, STARS), bf16),
            jax.ShapeDtypeStruct((32, STARS), f8),
            jax.ShapeDtypeStruct((8, 128), f32),
        ],
        in_specs=[vmem()] * 8 + [smem()],
        out_specs=[vmem()] * (PAIRS + 6),
        scratch_shapes=[
            pltpu.VMEM((16, STARS), f32),
            pltpu.SemaphoreType.DMA((PAIRS, 4, 4)),
            pltpu.SemaphoreType.DMA((PAIRS, 4, 4)),
        ],
        compiler_params=params(0),
        name="predict_gather",
    )(
        positions, velocities, old_acc, old_jerk, lines(masses), lines(elapsed), lines(levels),
        active_index, active_count,
    )
    parts = pl.pallas_call(
        pair_kernel,
        out_shape=[jax.ShapeDtypeStruct((OWNERS, 8, 128), f32)] * PAIRS,
        in_specs=[vmem()] * 8,
        out_specs=[vmem()] * PAIRS,
        scratch_shapes=[
            pltpu.VMEM((8, ROOM), f32),
            pltpu.VMEM((8, ROOM), f32),
            pltpu.VMEM((128, BLOCK), bf16),
            pltpu.VMEM((96, BLOCK), f32),
            pltpu.VMEM((8, 128), jnp.int32),
            pltpu.SMEM((8, 128), jnp.int32),
            pltpu.SemaphoreType.DMA,
        ],
        compiler_params=params(),
        name="pair_sums",
    )(*[e.reshape(OWNERS, 8, 128) for e in every], hq, hr, fw, fl, centre)

    def buffers(count, which):
        head = () if count is None else (count,)
        return [pltpu.VMEM(head + order[which] + (8, 128), f32) for order in REDUCE_ORDER]

    return pl.pallas_call(
        reduce_kernel,
        out_shape=jax.ShapeDtypeStruct((12, SLOTS), f32),
        in_specs=[vmem()] * (PAIRS + 1) + [smem()],
        out_specs=vmem(),
        scratch_shapes=[
            buffers(4, 1),
            buffers(3, 1),
            buffers(3, 2),
            [pltpu.VMEM((3, 8, 128), f32)] * PAIRS,
            buffers(4, 1),
            buffers(None, 2),
            pltpu.SemaphoreType.DMA((PAIRS, 4, 4)),
            pltpu.SemaphoreType.DMA((PAIRS, 4, 4)),
        ],
        compiler_params=params(1),
        name="reduce_correct",
    )(*[p.reshape(PLACES) for p in parts], start, active_count)


def solution(mesh):
    every = ("ia", "ja")
    in_specs = (
        P(None, every), P(None, every), P(None, every), P(None, every),
        P(every), P(every), P(every), P(every, None), P(every),
    )
    return jax.shard_map(
        shards, mesh=mesh, in_specs=in_specs, out_specs=P(None, every), check_vma=False
    )
```

```python
import jax
import jax.numpy as jnp
from jax import lax
from jax.experimental import pallas as pl
from jax.experimental.pallas import tpu as pltpu
from jax.sharding import PartitionSpec as P

MESH = pl.DeviceIdType.MESH
soften = 0.01
f32 = jnp.float32
bf16 = jnp.bfloat16
f8 = jnp.float8_e4m3fn

STARS = 1536
SLOTS = 512
OWNERS = 128
BLOCK = 256
CHUNK = 768
ROOM = OWNERS * SLOTS + SLOTS + 128
VMEM_LIMIT = 56 * 2**20
PAIRS = 3
GATHER_ORDER = ("xyz", "yzx", "zxy")
REDUCE_ORDER = (
    ("zyx", (2, 4, 2), (2, 2), lambda r, j: r.at[:, j], lambda r, j: r.at[j // 2, j % 2]),
    ("xzy", (4, 4), (4,), lambda r, j: r.at[j], lambda r, j: r.at[j]),
    ("yxz", (4, 2, 2), (4,), lambda r, j: r.at[:, j // 2, j % 2], lambda r, j: r.at[j]),
)
PLACES = (4, 2, 4, 2, 2, 8, 128)
POS_SCALE = 2.0**-2
VEL_SCALE = 2.0**-8
W_SCALE = 2.0**6


def vmem():
    return pl.BlockSpec(memory_space=pltpu.VMEM)


def smem():
    return pl.BlockSpec(memory_space=pltpu.SMEM)


def split3(x):
    a = x.astype(bf16).astype(f32)
    rest = x - a
    b = rest.astype(bf16).astype(f32)
    return a, b, rest - b


def place():
    ia, ja = lax.axis_index("ia"), lax.axis_index("ja")
    return {"z": ia // 2, "x": (ia % 2) * 2 + (ja // 2) % 2, "y": ja // 4}, ja % 2


def device(at, core):
    return (at["z"] * 2 + at["x"] // 2, at["y"] * 4 + (at["x"] % 2) * 2 + core)


def along(me, core, axis, d):
    return device({**me, axis: (me[axis] + d) % 4}, core)


def view(ref, at, core):
    xh, xl = (slice(None),) * 2 if at["x"] is None else (at["x"] // 2, at["x"] % 2)
    z = slice(None) if at["z"] is None else at["z"]
    y = slice(None) if at["y"] is None else at["y"]
    return ref.at[z, xh, y, xl, core]


def greet():
    me, core = place()
    barrier = pltpu.get_barrier_semaphore()
    peers = [along(me, core, axis, d) for axis in "xyz" for d in (1, 2, 3)]
    for peer in [device(me, 1 - core)] + peers:
        pl.semaphore_signal(barrier, inc=1, device_id=peer, device_id_type=MESH)
    return barrier


def predict(d, step):
    tau_sq = 0.5 * step * step
    tau_cube = step * step * step / 6.0
    pos = d[0:3] + step * d[3:6] + tau_sq * d[6:9] + tau_cube * d[9:12]
    vel = d[3:6] + step * d[6:9] + tau_sq * d[9:12]
    return pos, vel


def flat(ref):
    return jnp.concatenate([ref[i:i + 1, :] for i in range(STARS // 128)], axis=1)


def fold(rows):
    return jnp.concatenate([rows[:, 128 * t:128 * (t + 1)] for t in range(4)], axis=0)


def unfold(blocks):
    return jnp.concatenate(
        [jnp.concatenate([b[2 * t:2 * t + 2] for b in blocks], axis=0) for t in range(4)], axis=1
    )


def gather_kernel(
    pos_ref, vel_ref, acc_ref, jerk_ref, mass_ref, elapsed_ref, levels_ref, index_ref, count_ref,
    all0, all1, all2, start_ref, hq_ref, hr_ref, fw_ref, f8_ref, centre_ref,
    state, send_sem, recv_sem,
):
    every = (all0, all1, all2)
    barrier = greet()
    me, core = place()
    started = []

    def send(p, phase, k, block, target):
        c = pltpu.make_async_remote_copy(
            src_ref=block, dst_ref=block, send_sem=send_sem.at[p, phase, k],
            recv_sem=recv_sem.at[p, phase, k], device_id=target, device_id_type=MESH,
        )
        c.start()
        started.append(c)
        return c

    state[...] = jnp.zeros_like(state)
    state[0:3] = pos_ref[...]
    state[3:6] = vel_ref[...]
    state[6:9] = acc_ref[...]
    state[9:12] = jerk_ref[...]
    levels = flat(levels_ref)
    step = jnp.where(
        levels == 0, 0.5, jnp.where(levels == 1, 0.25, jnp.where(levels == 2, 0.125, 0.0625))
    ).astype(f32)
    state[12:13] = step

    pick = (lax.broadcasted_iota(jnp.int32, (STARS, SLOTS), 0) == index_ref[...]).astype(f32)
    pick = pick.astype(bf16)
    parts = jnp.concatenate(split3(state[...]), axis=0).astype(bf16)
    rows = jnp.dot(parts, pick, preferred_element_type=f32)
    start = (rows[0:16] + rows[16:32]) + rows[32:48]
    start_ref[...] = start
    target = jnp.concatenate(predict(start, start[12:13]), axis=0)
    live = lax.broadcasted_iota(jnp.int32, (8, SLOTS), 1) < count_ref[0]
    view(all0, me, core)[...] = fold(jnp.where(live[0:2], target[0:2], 1e30))
    view(all1, me, core)[...] = fold(target[2:4])
    view(all2, me, core)[...] = fold(target[4:6])

    pl.semaphore_wait(barrier, 10)

    have = [dict(me) for _ in range(PAIRS)]
    flight = [[] for _ in range(PAIRS)]

    def begin(phase):
        for p in range(PAIRS):
            axis = GATHER_ORDER[p][phase]
            flight[p] = [
                send(p, phase, d - 1, view(every[p], have[p], core), along(me, core, axis, d))
                for d in (1, 2, 3)
            ]

    def finish(phase):
        for p in range(PAIRS):
            for c in flight[p]:
                c.wait_recv()
            have[p][GATHER_ORDER[p][phase]] = None

    begin(0)
    chosen = lax.dot_general(
        live.astype(f32).astype(bf16), pick, (((1,), (1,)), ((), ())),
        preferred_element_type=f32,
    )[0:1]
    interval = jnp.where(chosen > 0.5, step, flat(elapsed_ref))
    src = jnp.concatenate(predict(state[...], interval), axis=0)
    finish(0)
    begin(1)

    centre = jnp.sum(src, axis=1, keepdims=True) * (1.0 / STARS)
    centre = jnp.floor(centre * 64.0 + 0.5) * (1.0 / 64.0)
    src = src - centre
    centre = jnp.concatenate([centre, jnp.zeros((2, 1), f32)], axis=0)
    centre_ref[...] = jnp.broadcast_to(centre, (8, 128))
    zero = jnp.zeros((1, STARS), f32)
    weights = jnp.concatenate([src, zero + 1.0, zero], axis=0) * flat(mass_ref)
    pos, vel = src[0:3] * POS_SCALE, src[3:6] * VEL_SCALE
    row = lax.broadcasted_iota(jnp.int32, (8, 1), 0)

    def factors(own, square, unit):
        a, b, c = split3(jnp.concatenate([own, zero, zero], axis=0))
        a = a + (row == unit).astype(f32)
        s = jnp.concatenate(split3(square) + (zero,) * 5, axis=0)
        fill = jnp.zeros((72, STARS), f32)
        return jnp.concatenate([a, b, a, b, c, a, s, fill], axis=0).T.astype(bf16)

    square = pos[0:1] * pos[0:1] + pos[1:2] * pos[1:2] + pos[2:3] * pos[2:3]
    hq_ref[...] = factors(jnp.concatenate([pos * -2.0, zero, zero, zero], axis=0), square, 6)
    finish(1)
    begin(2)
    over = [
        [send(p, 3, 0, view(every[p], have[p], core), device(me, 1 - core))]
        for p in range(PAIRS)
    ]
    product = pos[0:1] * vel[0:1] + pos[1:2] * vel[1:2] + pos[2:3] * vel[2:3]
    hr_ref[...] = factors(jnp.concatenate([-vel, -pos], axis=0), product, 7)
    fill = jnp.zeros((8, STARS), f32)
    fw_ref[...] = jnp.concatenate(split3(weights) + (fill,), axis=0).astype(bf16)
    high = weights.astype(f8).astype(f32)
    f8_ref[...] = jnp.concatenate([high, weights - high, fill, fill], axis=0).astype(f8)

    for d in (1, 2, 3):
        for p in range(PAIRS):
            axis = GATHER_ORDER[p][2]
            flight[p][d - 1].wait_recv()
            came = {**have[p], axis: (me[axis] - d + 4) % 4}
            over[p].append(send(p, 3, d, view(every[p], came, core), device(me, 1 - core)))
    for p in range(PAIRS):
        for c in over[p]:
            c.wait_recv()
    for c in started:
        c.wait_send()


def pair_kernel(
    all0, all1, all2, hq, hr, fw, fl, centre_ref,
    out0, out1, out2,
    comp, sums, factor, raw, counts, count, sem,
):
    outs = (out0, out1, out2)
    marked = jnp.where(all0[...] < 1e29, 0.5, 0.0)
    marked = jnp.sum(marked, axis=1).astype(bf16)
    counted = lax.dot_general(
        jnp.ones((8, 128), bf16), marked, (((1,), (1,)), ((), ())), preferred_element_type=f32
    )
    counts[...] = counted.astype(jnp.int32)
    copy = pltpu.make_async_copy(counts, count, sem)
    copy.start()
    copy.wait()

    lane = lax.broadcasted_iota(jnp.int32, (8, 128), 1)
    blank = jnp.zeros((2, SLOTS), f32)

    def pack(o, offset):
        shift = offset % 128
        base = pl.multiple_of(offset - shift, 128)
        x = jnp.concatenate([unfold((all0[o], all1[o], all2[o])), blank], axis=0)
        x = jnp.concatenate([x, jnp.zeros((8, 128), f32)], axis=1)
        x = pltpu.roll(x, shift, 1)
        first = pl.ds(base, 128)
        comp[:, first] = jnp.where(lane < shift, comp[:, first], x[:, 0:128])
        comp[:, pl.ds(base + 128, SLOTS)] = x[:, 128:]
        return offset + count[0, o]

    total = lax.fori_loop(0, OWNERS, pack, jnp.int32(0), unroll=16)
    blocks = (total + BLOCK - 1) // BLOCK
    centre = centre_ref[:, 0:1]
    row = lax.broadcasted_iota(jnp.int32, (8, 1), 0)
    scale = jnp.where(row < 3, POS_SCALE, VEL_SCALE)

    def columns(i):
        return pl.ds(pl.multiple_of(i * BLOCK, BLOCK), BLOCK)

    def make_factor(i):
        t = (comp[:, columns(i)] - centre) * scale
        square = t[0:1] * t[0:1] + t[1:2] * t[1:2] + t[2:3] * t[2:3] + soften * POS_SCALE**2
        product = t[0:1] * t[3:4] + t[1:2] * t[4:5] + t[2:3] * t[5:6]
        a, b, c = split3(jnp.concatenate([t[0:6], square, product], axis=0))
        ones = jnp.ones((8, BLOCK), f32)
        fill = jnp.zeros((72, BLOCK), f32)
        factor[...] = jnp.concatenate([a, a, b, b, a, c, ones, fill], axis=0).astype(bf16)

    def combine(i):
        sw = raw[0:8] + (raw[8:16] + raw[16:24]) + (raw[64:72] + raw[72:80])
        sb = raw[32:40] + (raw[40:48] + raw[48:56]) + (raw[80:88] + raw[88:96])
        t = comp[:, columns(i)] - centre
        rw = (sw - t * sw[6:7]) * (1.0 / W_SCALE)
        rb = pltpu.roll(sb - t * sb[6:7], 3, 0)
        sums[:, columns(i)] = rw - jnp.where((row >= 3) & (row < 6), 3.0 * rb, 0.0)

    def block(i, carry):
        combine(jnp.maximum(i - 1, 0))
        g = factor[...]
        sw = jnp.zeros((32, BLOCK), f32)
        sb = jnp.zeros((32, BLOCK), f32)
        lw = jnp.zeros((32, BLOCK), f32)
        lb = jnp.zeros((32, BLOCK), f32)
        for first in range(0, STARS, CHUNK):
            part = slice(first, first + CHUNK)
            q = jnp.dot(hq[part], g, preferred_element_type=f32)
            rv = jnp.dot(hr[part], g, preferred_element_type=f32)
            inv = lax.rsqrt(q)
            inv2 = inv * inv
            w = inv2 * inv
            b = w * inv2 * rv
            w_high = w.astype(bf16)
            b_high = b.astype(bf16)
            w_low = (w - w_high.astype(f32)).astype(f8)
            b_low = (b - b_high.astype(f32)).astype(f8)
            sw += jnp.dot(fw[:, part], w_high, preferred_element_type=f32)
            sb += jnp.dot(fw[:, part], b_high, preferred_element_type=f32)
            lw += jnp.dot(fl[:, part], w_low, preferred_element_type=f32)
            lb += jnp.dot(fl[:, part], b_low, preferred_element_type=f32)
        raw[0:32] = sw
        raw[32:64] = sb
        raw[64:80] = lw[0:16]
        raw[80:96] = lb[0:16]
        make_factor(i + 1)
        return carry

    raw[...] = jnp.zeros_like(raw)
    make_factor(0)
    lax.fori_loop(0, blocks, block, 0)
    combine(jnp.maximum(blocks - 1, 0))

    def unpack(o, offset):
        shift = offset % 128
        base = pl.multiple_of(offset - shift, 128)
        x = sums[:, pl.ds(base, SLOTS + 128)]
        x = pltpu.roll(x, (SLOTS + 128) - shift, 1)
        for p in range(PAIRS):
            outs[p][o] = fold(x[2 * p:2 * p + 2, 0:SLOTS])
        return offset + count[0, o]

    lax.fori_loop(0, OWNERS, unpack, jnp.int32(0), unroll=16)


def reduce_kernel(
    part0, part1, part2, start_ref, count_ref, out_ref,
    got_core, got_1, got_2, got_3, sum_1, sum_2, send_sem, recv_sem,
):
    part = (part0, part1, part2)
    barrier = greet()
    me, core = place()
    started = []

    def send(p, phase, k, src, dst, target):
        c = pltpu.make_async_remote_copy(
            src_ref=src, dst_ref=dst, send_sem=send_sem.at[p, phase, k],
            recv_sem=recv_sem.at[p, phase, k], device_id=target, device_id_type=MESH,
        )
        c.start()
        started.append(c)
        return c

    def plane(p, d):
        axis = REDUCE_ORDER[p][0][0]
        return {"x": None, "y": None, "z": None, axis: (me[axis] + d) % 4}

    pl.semaphore_wait(barrier, 10)
    over = [[None] * PAIRS for _ in range(5)]
    for d in (1, 2, 3, 4):
        for p in range(PAIRS):
            over[d][p] = send(
                p, 0, d - 1, view(part[p], plane(p, d), 1 - core), got_core[p].at[d - 1],
                device(me, 1 - core),
            )
    first = [[] for _ in range(PAIRS)]
    for d in (1, 2, 3, 4):
        for p in range(PAIRS):
            over[d][p].wait_recv()
            sum_1[p][d - 1] = view(part[p], plane(p, d), core)[...] + got_core[p][d - 1]
            if d < 4:
                axis = REDUCE_ORDER[p][0][0]
                first[p].append(send(
                    p, 1, d - 1, sum_1[p].at[d - 1], got_1[p].at[d - 1],
                    along(me, core, axis, d),
                ))
    second = [[] for _ in range(PAIRS)]
    for p in range(PAIRS):
        axes, _, _, at2, _ = REDUCE_ORDER[p]
        for c in first[p]:
            c.wait_recv()
        sum_1[p][3] = sum_1[p][3] + (got_1[p][0] + got_1[p][1] + got_1[p][2])
        for d in (1, 2, 3):
            second[p].append(send(
                p, 2, d - 1, at2(sum_1[p].at[3], (me[axes[1]] + d) % 4), got_2[p].at[d - 1],
                along(me, core, axes[1], d),
            ))
    third = [[] for _ in range(PAIRS)]
    for p in range(PAIRS):
        axes, _, _, at2, at3 = REDUCE_ORDER[p]
        for c in second[p]:
            c.wait_recv()
        own = at2(sum_1[p].at[3], me[axes[1]])[...]
        sum_2[p][...] = own + (got_2[p][0] + got_2[p][1] + got_2[p][2])
        for d in (1, 2, 3):
            third[p].append(send(
                p, 3, d - 1, at3(sum_2[p], (me[axes[2]] + d) % 4), got_3[p].at[d - 1],
                along(me, core, axes[2], d),
            ))
    blocks = []
    for p in range(PAIRS):
        axes, _, _, _, at3 = REDUCE_ORDER[p]
        for c in third[p]:
            c.wait_recv()
        own = at3(sum_2[p], me[axes[2]])[...]
        blocks.append(own + (got_3[p][0] + got_3[p][1] + got_3[p][2]))

    total = unfold(blocks) * (1.0 / (STARS * OWNERS))
    start = start_ref[...]
    step = start[12:13]
    acc0, jerk0 = start[6:9], start[9:12]
    acc1, jerk1 = total[0:3], total[3:6]
    vel1 = start[3:6] + (acc0 + acc1) * step / 2.0 + (jerk0 - jerk1) * step * step / 12.0
    pos1 = start[0:3] + (start[3:6] + vel1) * step / 2.0 + (acc0 - acc1) * step * step / 12.0
    state = jnp.concatenate([pos1, vel1, acc1, jerk1], axis=0)
    live = lax.broadcasted_iota(jnp.int32, (12, SLOTS), 1) < count_ref[0]
    out_ref[...] = jnp.where(live, state, 0.0)
    for c in started:
        c.wait_send()


def shards(
    positions, velocities, old_acc, old_jerk, masses, elapsed, levels, active_index, active_count
):
    def lines(a):
        return a.reshape(STARS // 128, 128)

    def params(collective_id=None):
        extra = {} if collective_id is None else {
            "collective_id": collective_id, "has_side_effects": True
        }
        return pltpu.CompilerParams(vmem_limit_bytes=VMEM_LIMIT, **extra)

    *every, start, hq, hr, fw, fl, centre = pl.pallas_call(
        gather_kernel,
        out_shape=[jax.ShapeDtypeStruct(PLACES, f32)] * PAIRS + [
            jax.ShapeDtypeStruct((16, SLOTS), f32),
            jax.ShapeDtypeStruct((STARS, 128), bf16),
            jax.ShapeDtypeStruct((STARS, 128), bf16),
            jax.ShapeDtypeStruct((32, STARS), bf16),
            jax.ShapeDtypeStruct((32, STARS), f8),
            jax.ShapeDtypeStruct((8, 128), f32),
        ],
        in_specs=[vmem()] * 8 + [smem()],
        out_specs=[vmem()] * (PAIRS + 6),
        scratch_shapes=[
            pltpu.VMEM((16, STARS), f32),
            pltpu.SemaphoreType.DMA((PAIRS, 4, 4)),
            pltpu.SemaphoreType.DMA((PAIRS, 4, 4)),
        ],
        compiler_params=params(0),
        name="predict_gather",
    )(
        positions, velocities, old_acc, old_jerk, lines(masses), lines(elapsed), lines(levels),
        active_index, active_count,
    )
    parts = pl.pallas_call(
        pair_kernel,
        out_shape=[jax.ShapeDtypeStruct((OWNERS, 8, 128), f32)] * PAIRS,
        in_specs=[vmem()] * 8,
        out_specs=[vmem()] * PAIRS,
        scratch_shapes=[
            pltpu.VMEM((8, ROOM), f32),
            pltpu.VMEM((8, ROOM), f32),
            pltpu.VMEM((128, BLOCK), bf16),
            pltpu.VMEM((96, BLOCK), f32),
            pltpu.VMEM((8, 128), jnp.int32),
            pltpu.SMEM((8, 128), jnp.int32),
            pltpu.SemaphoreType.DMA,
        ],
        compiler_params=params(),
        name="pair_sums",
    )(*[e.reshape(OWNERS, 8, 128) for e in every], hq, hr, fw, fl, centre)

    def buffers(count, which):
        head = () if count is None else (count,)
        return [pltpu.VMEM(head + order[which] + (8, 128), f32) for order in REDUCE_ORDER]

    return pl.pallas_call(
        reduce_kernel,
        out_shape=jax.ShapeDtypeStruct((12, SLOTS), f32),
        in_specs=[vmem()] * (PAIRS + 1) + [smem()],
        out_specs=vmem(),
        scratch_shapes=[
            buffers(4, 1),
            buffers(3, 1),
            buffers(3, 2),
            [pltpu.VMEM((3, 8, 128), f32)] * PAIRS,
            buffers(4, 1),
            buffers(None, 2),
            pltpu.SemaphoreType.DMA((PAIRS, 4, 4)),
            pltpu.SemaphoreType.DMA((PAIRS, 4, 4)),
        ],
        compiler_params=params(1),
        name="reduce_correct",
    )(*[p.reshape(PLACES) for p in parts], start, active_count)


def solution(mesh):
    every = ("ia", "ja")
    in_specs = (
        P(None, every), P(None, every), P(None, every), P(None, every),
        P(every), P(every), P(every), P(every, None), P(every),
    )
    return jax.shard_map(
        shards, mesh=mesh, in_specs=in_specs, out_specs=P(None, every), check_vma=False
    )
```

```python
import jax
import jax.numpy as jnp
from jax import lax
from jax.experimental import pallas as pl
from jax.experimental.pallas import tpu as pltpu
from jax.sharding import PartitionSpec as P

MESH = pl.DeviceIdType.MESH
soften = 0.01
f32 = jnp.float32
bf16 = jnp.bfloat16
f8 = jnp.float8_e4m3fn

STARS = 1536
SLOTS = 512
OWNERS = 128
BLOCK = 256
CHUNK = 256
ROOM = OWNERS * SLOTS + SLOTS + 128
VMEM_LIMIT = 56 * 2**20
PAIRS = 3
GATHER_ORDER = ("xyz", "yzx", "zxy")
REDUCE_ORDER = (
    ("zyx", (2, 4, 2), (2, 2), lambda r, j: r.at[:, j], lambda r, j: r.at[j // 2, j % 2]),
    ("xzy", (4, 4), (4,), lambda r, j: r.at[j], lambda r, j: r.at[j]),
    ("yxz", (4, 2, 2), (4,), lambda r, j: r.at[:, j // 2, j % 2], lambda r, j: r.at[j]),
)
PLACES = (4, 2, 4, 2, 2, 8, 128)
POS_SCALE = 2.0**-2
VEL_SCALE = 2.0**-8
W_SCALE = 2.0**6


def vmem():
    return pl.BlockSpec(memory_space=pltpu.VMEM)


def smem():
    return pl.BlockSpec(memory_space=pltpu.SMEM)


def split3(x):
    a = x.astype(bf16).astype(f32)
    rest = x - a
    b = rest.astype(bf16).astype(f32)
    return a, b, rest - b


def place():
    ia, ja = lax.axis_index("ia"), lax.axis_index("ja")
    return {"z": ia // 2, "x": (ia % 2) * 2 + (ja // 2) % 2, "y": ja // 4}, ja % 2


def device(at, core):
    return (at["z"] * 2 + at["x"] // 2, at["y"] * 4 + (at["x"] % 2) * 2 + core)


def along(me, core, axis, d):
    return device({**me, axis: (me[axis] + d) % 4}, core)


def view(ref, at, core):
    xh, xl = (slice(None),) * 2 if at["x"] is None else (at["x"] // 2, at["x"] % 2)
    z = slice(None) if at["z"] is None else at["z"]
    y = slice(None) if at["y"] is None else at["y"]
    return ref.at[z, xh, y, xl, core]


def greet():
    me, core = place()
    barrier = pltpu.get_barrier_semaphore()
    peers = [along(me, core, axis, d) for axis in "xyz" for d in (1, 2, 3)]
    for peer in [device(me, 1 - core)] + peers:
        pl.semaphore_signal(barrier, inc=1, device_id=peer, device_id_type=MESH)
    return barrier


def predict(d, step):
    tau_sq = 0.5 * step * step
    tau_cube = step * step * step / 6.0
    pos = d[0:3] + step * d[3:6] + tau_sq * d[6:9] + tau_cube * d[9:12]
    vel = d[3:6] + step * d[6:9] + tau_sq * d[9:12]
    return pos, vel


def flat(ref):
    return jnp.concatenate([ref[i:i + 1, :] for i in range(STARS // 128)], axis=1)


def fold(rows):
    return jnp.concatenate([rows[:, 128 * t:128 * (t + 1)] for t in range(4)], axis=0)


def unfold(blocks):
    return jnp.concatenate(
        [jnp.concatenate([b[2 * t:2 * t + 2] for b in blocks], axis=0) for t in range(4)], axis=1
    )


def gather_kernel(
    pos_ref, vel_ref, acc_ref, jerk_ref, mass_ref, elapsed_ref, levels_ref, index_ref, count_ref,
    all0, all1, all2, start_ref, hq_ref, hr_ref, fw_ref, f8_ref, centre_ref,
    state, send_sem, recv_sem,
):
    every = (all0, all1, all2)
    barrier = greet()
    me, core = place()
    started = []

    def send(p, phase, k, block, target):
        c = pltpu.make_async_remote_copy(
            src_ref=block, dst_ref=block, send_sem=send_sem.at[p, phase, k],
            recv_sem=recv_sem.at[p, phase, k], device_id=target, device_id_type=MESH,
        )
        c.start()
        started.append(c)
        return c

    state[...] = jnp.zeros_like(state)
    state[0:3] = pos_ref[...]
    state[3:6] = vel_ref[...]
    state[6:9] = acc_ref[...]
    state[9:12] = jerk_ref[...]
    levels = flat(levels_ref)
    step = jnp.where(
        levels == 0, 0.5, jnp.where(levels == 1, 0.25, jnp.where(levels == 2, 0.125, 0.0625))
    ).astype(f32)
    state[12:13] = step

    pick = (lax.broadcasted_iota(jnp.int32, (STARS, SLOTS), 0) == index_ref[...]).astype(f32)
    pick = pick.astype(bf16)
    parts = jnp.concatenate(split3(state[...]), axis=0).astype(bf16)
    rows = jnp.dot(parts, pick, preferred_element_type=f32)
    start = (rows[0:16] + rows[16:32]) + rows[32:48]
    start_ref[...] = start
    target = jnp.concatenate(predict(start, start[12:13]), axis=0)
    live = lax.broadcasted_iota(jnp.int32, (8, SLOTS), 1) < count_ref[0]
    view(all0, me, core)[...] = fold(jnp.where(live[0:2], target[0:2], 1e30))
    view(all1, me, core)[...] = fold(target[2:4])
    view(all2, me, core)[...] = fold(target[4:6])

    pl.semaphore_wait(barrier, 10)

    have = [dict(me) for _ in range(PAIRS)]
    flight = [[] for _ in range(PAIRS)]

    def begin(phase):
        for p in range(PAIRS):
            axis = GATHER_ORDER[p][phase]
            flight[p] = [
                send(p, phase, d - 1, view(every[p], have[p], core), along(me, core, axis, d))
                for d in (1, 2, 3)
            ]

    def finish(phase):
        for p in range(PAIRS):
            for c in flight[p]:
                c.wait_recv()
            have[p][GATHER_ORDER[p][phase]] = None

    begin(0)
    chosen = lax.dot_general(
        live.astype(f32).astype(bf16), pick, (((1,), (1,)), ((), ())),
        preferred_element_type=f32,
    )[0:1]
    interval = jnp.where(chosen > 0.5, step, flat(elapsed_ref))
    src = jnp.concatenate(predict(state[...], interval), axis=0)
    finish(0)
    begin(1)

    centre = jnp.sum(src, axis=1, keepdims=True) * (1.0 / STARS)
    centre = jnp.floor(centre * 64.0 + 0.5) * (1.0 / 64.0)
    src = src - centre
    centre = jnp.concatenate([centre, jnp.zeros((2, 1), f32)], axis=0)
    centre_ref[...] = jnp.broadcast_to(centre, (8, 128))
    zero = jnp.zeros((1, STARS), f32)
    weights = jnp.concatenate([src, zero + 1.0, zero], axis=0) * flat(mass_ref)
    pos, vel = src[0:3] * POS_SCALE, src[3:6] * VEL_SCALE
    row = lax.broadcasted_iota(jnp.int32, (8, 1), 0)

    def factors(own, square, unit):
        a, b, c = split3(jnp.concatenate([own, zero, zero], axis=0))
        a = a + (row == unit).astype(f32)
        s = jnp.concatenate(split3(square) + (zero,) * 5, axis=0)
        fill = jnp.zeros((72, STARS), f32)
        return jnp.concatenate([a, b, a, b, c, a, s, fill], axis=0).T.astype(bf16)

    square = pos[0:1] * pos[0:1] + pos[1:2] * pos[1:2] + pos[2:3] * pos[2:3]
    hq_ref[...] = factors(jnp.concatenate([pos * -2.0, zero, zero, zero], axis=0), square, 6)
    finish(1)
    begin(2)
    over = [
        [send(p, 3, 0, view(every[p], have[p], core), device(me, 1 - core))]
        for p in range(PAIRS)
    ]
    product = pos[0:1] * vel[0:1] + pos[1:2] * vel[1:2] + pos[2:3] * vel[2:3]
    hr_ref[...] = factors(jnp.concatenate([-vel, -pos], axis=0), product, 7)
    fill = jnp.zeros((8, STARS), f32)
    fw_ref[...] = jnp.concatenate(split3(weights)[0:2], axis=0).astype(bf16)
    high = weights.astype(f8).astype(f32)
    f8_ref[...] = jnp.concatenate([high, weights - high, fill, fill], axis=0).astype(f8)

    for d in (1, 2, 3):
        for p in range(PAIRS):
            axis = GATHER_ORDER[p][2]
            flight[p][d - 1].wait_recv()
            came = {**have[p], axis: (me[axis] - d + 4) % 4}
            over[p].append(send(p, 3, d, view(every[p], came, core), device(me, 1 - core)))
    for p in range(PAIRS):
        for c in over[p]:
            c.wait_recv()
    for c in started:
        c.wait_send()


def pair_kernel(
    all0, all1, all2, hq, hr, fw, fl, centre_ref,
    out0, out1, out2,
    comp, sums, factor, raw, counts, count, sem,
):
    outs = (out0, out1, out2)
    marked = jnp.where(all0[...] < 1e29, 0.5, 0.0)
    counted = jnp.sum(jnp.sum(marked, axis=1), axis=1, keepdims=True)
    counted = jnp.broadcast_to(counted, (OWNERS, 128)).T[0:8]
    counts[...] = counted.astype(jnp.int32)
    copy = pltpu.make_async_copy(counts, count, sem)
    copy.start()
    copy.wait()

    lane = lax.broadcasted_iota(jnp.int32, (8, 128), 1)
    blank = jnp.zeros((2, SLOTS), f32)

    def pack(o, offset):
        shift = offset % 128
        base = pl.multiple_of(offset - shift, 128)
        x = jnp.concatenate([unfold((all0[o], all1[o], all2[o])), blank], axis=0)
        x = jnp.concatenate([x, jnp.zeros((8, 128), f32)], axis=1)
        x = pltpu.roll(x, shift, 1)
        first = pl.ds(base, 128)
        comp[:, first] = jnp.where(lane < shift, comp[:, first], x[:, 0:128])
        comp[:, pl.ds(base + 128, SLOTS)] = x[:, 128:]
        return offset + count[0, o]

    total = lax.fori_loop(0, OWNERS, pack, jnp.int32(0), unroll=16)
    blocks = (total + BLOCK - 1) // BLOCK
    centre = centre_ref[:, 0:1]
    row = lax.broadcasted_iota(jnp.int32, (8, 1), 0)
    scale = jnp.where(row < 3, POS_SCALE, VEL_SCALE)

    def columns(i):
        return pl.ds(pl.multiple_of(i * BLOCK, BLOCK), BLOCK)

    def make_factor(i):
        t = (comp[:, columns(i)] - centre) * scale
        square = t[0:1] * t[0:1] + t[1:2] * t[1:2] + t[2:3] * t[2:3] + soften * POS_SCALE**2
        product = t[0:1] * t[3:4] + t[1:2] * t[4:5] + t[2:3] * t[5:6]
        a, b, c = split3(jnp.concatenate([t[0:6], square, product], axis=0))
        ones = jnp.ones((8, BLOCK), f32)
        fill = jnp.zeros((200, BLOCK), f32)
        factor[...] = jnp.concatenate([a, a, b, b, a, c, ones, fill], axis=0).astype(bf16)

    def combine(i):
        sw = raw[0:8] + (raw[8:16] + (raw[32:40] + raw[40:48]))
        sb = raw[16:24] + (raw[24:32] + (raw[64:72] + raw[72:80]))
        t = comp[:, columns(i)] - centre
        rw = (sw - t * sw[6:7]) * (1.0 / W_SCALE)
        rb = pltpu.roll(sb - t * sb[6:7], 3, 0)
        sums[:, columns(i)] = rw - jnp.where((row >= 3) & (row < 6), 3.0 * rb, 0.0)

    def products(acc_q, acc_r, acc_w, acc_b, acc_lw, acc_lb):
        def stage_one(c, buffer, load):
            part = slice(c * CHUNK, (c + 1) * CHUNK)
            blank = jnp.zeros((CHUNK, 128), bf16)
            pltpu.matmul_acc_lhs(
                acc_q[buffer], jnp.concatenate([hq[part], blank], axis=1), load_staged_rhs=load
            )
            pltpu.matmul_acc_lhs(acc_r[buffer], jnp.concatenate([hr[part], blank], axis=1))

        def stage_factor(i):
            make_factor(i)
            pltpu.matmul_push_rhs(factor[...], 0, 0)

        def pop_sums():
            raw[0:16] = pltpu.matmul_pop(acc_w)
            raw[16:32] = pltpu.matmul_pop(acc_b)
            raw[32:64] = pltpu.matmul_pop(acc_lw)
            raw[64:96] = pltpu.matmul_pop(acc_lb)

        chunks = STARS // CHUNK

        def block(i, carry):
            for c in range(chunks):
                if c == chunks - 1:
                    stage_factor(i + 1)
                    stage_one(0, 0, 0)
                else:
                    stage_one(c + 1, (c + 1) % 2, None)
                q = pltpu.matmul_pop(acc_q[c % 2])
                rv = pltpu.matmul_pop(acc_r[c % 2])
                inv = lax.rsqrt(q)
                inv2 = inv * inv
                w = inv2 * inv
                b = w * inv2 * rv
                w_high = w.astype(bf16)
                b_high = b.astype(bf16)
                w_low = (w - w_high.astype(f32)).astype(f8)
                b_low = (b - b_high.astype(f32)).astype(f8)
                if c == 0:
                    pop_sums()
                part = slice(c * CHUNK, (c + 1) * CHUNK)
                pltpu.matmul_push_rhs(w_high, 0, 1)
                pltpu.matmul_acc_lhs(acc_w, fw[:, part], load_staged_rhs=0)
                pltpu.matmul_push_rhs(b_high, 1, 1)
                pltpu.matmul_acc_lhs(acc_b, fw[:, part], load_staged_rhs=1)
                pltpu.matmul_push_rhs(w_low, 0, 1)
                pltpu.matmul_acc_lhs(acc_lw, fl[:, part], load_staged_rhs=0)
                pltpu.matmul_push_rhs(b_low, 1, 1)
                pltpu.matmul_acc_lhs(acc_lb, fl[:, part], load_staged_rhs=1)
                if c == 0:
                    combine(jnp.maximum(i - 1, 0))
            return carry

        pop_sums()
        for k in range(2):
            pltpu.matmul_pop(acc_q[k])
            pltpu.matmul_pop(acc_r[k])
        stage_factor(0)
        stage_one(0, 0, 0)
        lax.fori_loop(0, blocks, block, 0)
        pltpu.matmul_pop(acc_q[0])
        pltpu.matmul_pop(acc_r[0])
        pop_sums()
        combine(jnp.maximum(blocks - 1, 0))

    pl.run_scoped(
        products,
        [pltpu.ACC(0)((CHUNK, BLOCK), f32)] * 2,
        [pltpu.ACC(0)((CHUNK, BLOCK), f32)] * 2,
        *[pltpu.ACC(1)((16, BLOCK), f32)] * 2,
        *[pltpu.ACC(1)((32, BLOCK), f32)] * 2,
    )

    def unpack(o, offset):
        shift = offset % 128
        base = pl.multiple_of(offset - shift, 128)
        x = sums[:, pl.ds(base, SLOTS + 128)]
        x = pltpu.roll(x, (SLOTS + 128) - shift, 1)
        for p in range(PAIRS):
            outs[p][o] = fold(x[2 * p:2 * p + 2, 0:SLOTS])
        return offset + count[0, o]

    lax.fori_loop(0, OWNERS, unpack, jnp.int32(0), unroll=16)


def pair_scratch():
    return [
        pltpu.VMEM((8, ROOM), f32),
        pltpu.VMEM((8, ROOM), f32),
        pltpu.VMEM((256, BLOCK), bf16),
        pltpu.VMEM((96, BLOCK), f32),
        pltpu.VMEM((8, 128), jnp.int32),
        pltpu.SMEM((8, 128), jnp.int32),
        pltpu.SemaphoreType.DMA,
    ]


def reduce_kernel(
    part0, part1, part2, start_ref, count_ref, out_ref,
    got_core, got_1, got_2, got_3, sum_1, sum_2, send_sem, recv_sem,
):
    part = (part0, part1, part2)
    barrier = greet()
    me, core = place()
    started = []

    def send(p, phase, k, src, dst, target):
        c = pltpu.make_async_remote_copy(
            src_ref=src, dst_ref=dst, send_sem=send_sem.at[p, phase, k],
            recv_sem=recv_sem.at[p, phase, k], device_id=target, device_id_type=MESH,
        )
        c.start()
        started.append(c)
        return c

    def plane(p, d):
        axis = REDUCE_ORDER[p][0][0]
        return {"x": None, "y": None, "z": None, axis: (me[axis] + d) % 4}

    pl.semaphore_wait(barrier, 10)
    over = [[None] * PAIRS for _ in range(5)]
    for d in (1, 2, 3, 4):
        for p in range(PAIRS):
            over[d][p] = send(
                p, 0, d - 1, view(part[p], plane(p, d), 1 - core), got_core[p].at[d - 1],
                device(me, 1 - core),
            )
    first = [[] for _ in range(PAIRS)]
    for d in (1, 2, 3, 4):
        for p in range(PAIRS):
            over[d][p].wait_recv()
            sum_1[p][d - 1] = view(part[p], plane(p, d), core)[...] + got_core[p][d - 1]
            if d < 4:
                axis = REDUCE_ORDER[p][0][0]
                first[p].append(send(
                    p, 1, d - 1, sum_1[p].at[d - 1], got_1[p].at[d - 1],
                    along(me, core, axis, d),
                ))
    second = [[] for _ in range(PAIRS)]
    for p in range(PAIRS):
        axes, _, _, at2, _ = REDUCE_ORDER[p]
        for c in first[p]:
            c.wait_recv()
        sum_1[p][3] = sum_1[p][3] + (got_1[p][0] + got_1[p][1] + got_1[p][2])
        for d in (1, 2, 3):
            second[p].append(send(
                p, 2, d - 1, at2(sum_1[p].at[3], (me[axes[1]] + d) % 4), got_2[p].at[d - 1],
                along(me, core, axes[1], d),
            ))
    third = [[] for _ in range(PAIRS)]
    for p in range(PAIRS):
        axes, _, _, at2, at3 = REDUCE_ORDER[p]
        for c in second[p]:
            c.wait_recv()
        own = at2(sum_1[p].at[3], me[axes[1]])[...]
        sum_2[p][...] = own + (got_2[p][0] + got_2[p][1] + got_2[p][2])
        for d in (1, 2, 3):
            third[p].append(send(
                p, 3, d - 1, at3(sum_2[p], (me[axes[2]] + d) % 4), got_3[p].at[d - 1],
                along(me, core, axes[2], d),
            ))
    blocks = []
    for p in range(PAIRS):
        axes, _, _, _, at3 = REDUCE_ORDER[p]
        for c in third[p]:
            c.wait_recv()
        own = at3(sum_2[p], me[axes[2]])[...]
        blocks.append(own + (got_3[p][0] + got_3[p][1] + got_3[p][2]))

    total = unfold(blocks) * (1.0 / (STARS * OWNERS))
    start = start_ref[...]
    step = start[12:13]
    acc0, jerk0 = start[6:9], start[9:12]
    acc1, jerk1 = total[0:3], total[3:6]
    vel1 = start[3:6] + (acc0 + acc1) * step / 2.0 + (jerk0 - jerk1) * step * step / 12.0
    pos1 = start[0:3] + (start[3:6] + vel1) * step / 2.0 + (acc0 - acc1) * step * step / 12.0
    state = jnp.concatenate([pos1, vel1, acc1, jerk1], axis=0)
    live = lax.broadcasted_iota(jnp.int32, (12, SLOTS), 1) < count_ref[0]
    out_ref[...] = jnp.where(live, state, 0.0)
    for c in started:
        c.wait_send()


def shards(
    positions, velocities, old_acc, old_jerk, masses, elapsed, levels, active_index, active_count
):
    def lines(a):
        return a.reshape(STARS // 128, 128)

    def params(collective_id=None):
        extra = {} if collective_id is None else {
            "collective_id": collective_id, "has_side_effects": True
        }
        return pltpu.CompilerParams(vmem_limit_bytes=VMEM_LIMIT, **extra)

    *every, start, hq, hr, fw, fl, centre = pl.pallas_call(
        gather_kernel,
        out_shape=[jax.ShapeDtypeStruct(PLACES, f32)] * PAIRS + [
            jax.ShapeDtypeStruct((16, SLOTS), f32),
            jax.ShapeDtypeStruct((STARS, 128), bf16),
            jax.ShapeDtypeStruct((STARS, 128), bf16),
            jax.ShapeDtypeStruct((16, STARS), bf16),
            jax.ShapeDtypeStruct((32, STARS), f8),
            jax.ShapeDtypeStruct((8, 128), f32),
        ],
        in_specs=[vmem()] * 8 + [smem()],
        out_specs=[vmem()] * (PAIRS + 6),
        scratch_shapes=[
            pltpu.VMEM((16, STARS), f32),
            pltpu.SemaphoreType.DMA((PAIRS, 4, 4)),
            pltpu.SemaphoreType.DMA((PAIRS, 4, 4)),
        ],
        compiler_params=params(0),
        name="predict_gather",
    )(
        positions, velocities, old_acc, old_jerk, lines(masses), lines(elapsed), lines(levels),
        active_index, active_count,
    )
    parts = pl.pallas_call(
        pair_kernel,
        out_shape=[jax.ShapeDtypeStruct((OWNERS, 8, 128), f32)] * PAIRS,
        in_specs=[vmem()] * 8,
        out_specs=[vmem()] * PAIRS,
        scratch_shapes=pair_scratch(),
        compiler_params=params(),
        name="pair_sums",
    )(*[e.reshape(OWNERS, 8, 128) for e in every], hq, hr, fw, fl, centre)

    def buffers(count, which):
        head = () if count is None else (count,)
        return [pltpu.VMEM(head + order[which] + (8, 128), f32) for order in REDUCE_ORDER]

    return pl.pallas_call(
        reduce_kernel,
        out_shape=jax.ShapeDtypeStruct((12, SLOTS), f32),
        in_specs=[vmem()] * (PAIRS + 1) + [smem()],
        out_specs=vmem(),
        scratch_shapes=[
            buffers(4, 1),
            buffers(3, 1),
            buffers(3, 2),
            [pltpu.VMEM((3, 8, 128), f32)] * PAIRS,
            buffers(4, 1),
            buffers(None, 2),
            pltpu.SemaphoreType.DMA((PAIRS, 4, 4)),
            pltpu.SemaphoreType.DMA((PAIRS, 4, 4)),
        ],
        compiler_params=params(1),
        name="reduce_correct",
    )(*[p.reshape(PLACES) for p in parts], start, active_count)


def solution(mesh):
    every = ("ia", "ja")
    in_specs = (
        P(None, every), P(None, every), P(None, every), P(None, every),
        P(every), P(every), P(every), P(every, None), P(every),
    )
    return jax.shard_map(
        shards, mesh=mesh, in_specs=in_specs, out_specs=P(None, every), check_vma=False
    )
```

```python
import jax
import jax.numpy as jnp
from jax import lax
from jax.experimental import pallas as pl
from jax.experimental.pallas import tpu as pltpu
from jax.sharding import PartitionSpec as P

MESH = pl.DeviceIdType.MESH
soften = 0.01
f32 = jnp.float32
bf16 = jnp.bfloat16
f8 = jnp.float8_e4m3fn

STARS = 1536
SLOTS = 512
OWNERS = 128
BLOCK = 256
CHUNK = 256
ROOM = OWNERS * SLOTS + SLOTS + 128
VMEM_LIMIT = 24 * 2**20
PAIRS = 3
AXES = ("xyz", "yzx", "zxy")
PLACES = (2, 4, 16, 8, 128)
POS_SCALE = 2.0**-2
VEL_SCALE = 2.0**-8
W_SCALE = 2.0**6


def vmem():
    return pl.BlockSpec(memory_space=pltpu.VMEM)


def smem():
    return pl.BlockSpec(memory_space=pltpu.SMEM)


def split3(x):
    a = x.astype(bf16).astype(f32)
    rest = x - a
    b = rest.astype(bf16).astype(f32)
    return a, b, rest - b


def place():
    ia, ja = lax.axis_index("ia"), lax.axis_index("ja")
    return {"z": ia // 2, "x": (ia % 2) * 2 + (ja // 2) % 2, "y": ja // 4}, ja % 2


def device(at, core):
    return (at["z"] * 2 + at["x"] // 2, at["y"] * 4 + (at["x"] % 2) * 2 + core)


def along(me, core, axis, d):
    return device({**me, axis: (me[axis] + d) % 4}, core)


def greet():
    me, core = place()
    barrier = pltpu.get_barrier_semaphore()
    peers = [along(me, core, axis, d) for axis in "xyz" for d in (1, 2, 3)]
    for peer in [device(me, 1 - core)] + peers:
        pl.semaphore_signal(barrier, inc=1, device_id=peer, device_id_type=MESH)
    return barrier


def predict(d, step):
    tau_sq = 0.5 * step * step
    tau_cube = step * step * step / 6.0
    pos = d[0:3] + step * d[3:6] + tau_sq * d[6:9] + tau_cube * d[9:12]
    vel = d[3:6] + step * d[6:9] + tau_sq * d[9:12]
    return pos, vel


def flat(ref):
    return jnp.concatenate([ref[i:i + 1, :] for i in range(STARS // 128)], axis=1)


def fold(rows):
    return jnp.concatenate([rows[:, 128 * t:128 * (t + 1)] for t in range(4)], axis=0)


def unfold(blocks):
    return jnp.concatenate(
        [jnp.concatenate([b[2 * t:2 * t + 2] for b in blocks], axis=0) for t in range(4)], axis=1
    )


def gather_kernel(
    pos_ref, vel_ref, acc_ref, jerk_ref, mass_ref, elapsed_ref, levels_ref, index_ref, count_ref,
    all0, all1, all2, start_ref, hq_ref, hr_ref, fw_ref, f8_ref, centre_ref,
    state, send_sem, recv_sem,
):
    every = (all0, all1, all2)
    barrier = greet()
    me, core = place()
    started = []

    def send(p, phase, k, block, target):
        c = pltpu.make_async_remote_copy(
            src_ref=block, dst_ref=block, send_sem=send_sem.at[p, phase, k],
            recv_sem=recv_sem.at[p, phase, k], device_id=target, device_id_type=MESH,
        )
        c.start()
        started.append(c)
        return c

    state[...] = jnp.zeros_like(state)
    state[0:3] = pos_ref[...]
    state[3:6] = vel_ref[...]
    state[6:9] = acc_ref[...]
    state[9:12] = jerk_ref[...]
    levels = flat(levels_ref)
    step = jnp.where(
        levels == 0, 0.5, jnp.where(levels == 1, 0.25, jnp.where(levels == 2, 0.125, 0.0625))
    ).astype(f32)
    state[12:13] = step

    pick = (lax.broadcasted_iota(jnp.int32, (STARS, SLOTS), 0) == index_ref[...]).astype(f32)
    pick = pick.astype(bf16)
    parts = jnp.concatenate(split3(state[...]), axis=0).astype(bf16)
    rows = jnp.dot(parts, pick, preferred_element_type=f32)
    start = (rows[0:16] + rows[16:32]) + rows[32:48]
    start_ref[...] = start
    target = jnp.concatenate(predict(start, start[12:13]), axis=0)
    live = lax.broadcasted_iota(jnp.int32, (8, SLOTS), 1) < count_ref[0]
    pairs = (jnp.where(live[0:2], target[0:2], 1e30), target[2:4], target[4:6])
    for p in range(PAIRS):
        one, two, three = (me[axis] for axis in AXES[p])
        every[p][core, three, one * 4 + two] = fold(pairs[p])

    pl.semaphore_wait(barrier, 10)

    flight = [[] for _ in range(PAIRS)]

    def begin(phase):
        for p in range(PAIRS):
            one, two, three = (me[axis] for axis in AXES[p])
            block = every[p].at[core, three]
            if phase == 0:
                block = block.at[one * 4 + two]
            elif phase == 1:
                block = block.at[pl.ds(one * 4, 4)]
            axis = AXES[p][(1, 0, 2)[phase]]
            flight[p] = [
                send(p, phase, d - 1, block, along(me, core, axis, d)) for d in (1, 2, 3)
            ]

    def finish():
        for p in range(PAIRS):
            for c in flight[p]:
                c.wait_recv()

    begin(0)
    chosen = lax.dot_general(
        live.astype(f32).astype(bf16), pick, (((1,), (1,)), ((), ())),
        preferred_element_type=f32,
    )[0:1]
    interval = jnp.where(chosen > 0.5, step, flat(elapsed_ref))
    src = jnp.concatenate(predict(state[...], interval), axis=0)
    finish()
    begin(1)

    centre = jnp.sum(src, axis=1, keepdims=True) * (1.0 / STARS)
    centre = jnp.floor(centre * 64.0 + 0.5) * (1.0 / 64.0)
    src = src - centre
    centre = jnp.concatenate([centre, jnp.zeros((2, 1), f32)], axis=0)
    centre_ref[...] = jnp.broadcast_to(centre, (8, 128))
    zero = jnp.zeros((1, STARS), f32)
    weights = jnp.concatenate([src, zero + 1.0, zero], axis=0) * flat(mass_ref)
    pos, vel = src[0:3] * POS_SCALE, src[3:6] * VEL_SCALE
    row = lax.broadcasted_iota(jnp.int32, (8, 1), 0)

    def factors(own, square, unit):
        a, b, c = split3(jnp.concatenate([own, zero, zero], axis=0))
        a = a + (row == unit).astype(f32)
        s = jnp.concatenate(split3(square) + (zero,) * 5, axis=0)
        fill = jnp.zeros((72, STARS), f32)
        return jnp.concatenate([a, b, a, b, c, a, s, fill], axis=0).T.astype(bf16)

    square = pos[0:1] * pos[0:1] + pos[1:2] * pos[1:2] + pos[2:3] * pos[2:3]
    hq_ref[...] = factors(jnp.concatenate([pos * -2.0, zero, zero, zero], axis=0), square, 6)
    finish()
    begin(2)
    over = [
        [send(p, 3, 0, every[p].at[core, me[AXES[p][2]]], device(me, 1 - core))]
        for p in range(PAIRS)
    ]
    product = pos[0:1] * vel[0:1] + pos[1:2] * vel[1:2] + pos[2:3] * vel[2:3]
    hr_ref[...] = factors(jnp.concatenate([-vel, -pos], axis=0), product, 7)
    fill = jnp.zeros((8, STARS), f32)
    fw_ref[...] = jnp.concatenate(split3(weights)[0:2], axis=0).astype(bf16)
    high = weights.astype(f8).astype(f32)
    f8_ref[...] = jnp.concatenate([high, weights - high, fill, fill], axis=0).astype(f8)

    for d in (1, 2, 3):
        for p in range(PAIRS):
            flight[p][d - 1].wait_recv()
            came = (me[AXES[p][2]] - d + 4) % 4
            over[p].append(send(p, 3, d, every[p].at[core, came], device(me, 1 - core)))
    for p in range(PAIRS):
        for c in over[p]:
            c.wait_recv()
    for c in started:
        c.wait_send()


def pair_kernel(
    all0, all1, all2, hq, hr, fw, fl, centre_ref,
    out0, out1, out2,
    comp, sums, factor, raw, counts, count, sem,
):
    outs = (out0, out1, out2)
    marked = jnp.where(all0[...] < 1e29, 0.5, 0.0)
    counted = jnp.sum(jnp.sum(marked, axis=1), axis=1, keepdims=True)
    counted = jnp.broadcast_to(counted, (OWNERS, 128)).T[0:8]
    counts[...] = counted.astype(jnp.int32)
    copy = pltpu.make_async_copy(counts, count, sem)
    copy.start()
    copy.wait()

    lane = lax.broadcasted_iota(jnp.int32, (8, 128), 1)
    blank = jnp.zeros((2, SLOTS), f32)

    def owners(step):
        def some(g, offset):
            core, z = g // 4, g % 4
            for x in range(4):
                for y in range(4):
                    at = {"x": x, "y": y, "z": z}
                    where = [
                        core * 64 + at[three] * 16 + at[one] * 4 + at[two]
                        for one, two, three in AXES
                    ]
                    offset = step(where, offset)
            return offset

        return lax.fori_loop(0, 8, some, jnp.int32(0))

    def pack(where, offset):
        shift = offset % 128
        base = pl.multiple_of(offset - shift, 128)
        x = unfold([ref[k] for ref, k in zip((all0, all1, all2), where)])
        x = jnp.concatenate([x, blank], axis=0)
        x = jnp.concatenate([x, jnp.zeros((8, 128), f32)], axis=1)
        x = pltpu.roll(x, shift, 1)
        first = pl.ds(base, 128)
        comp[:, first] = jnp.where(lane < shift, comp[:, first], x[:, 0:128])
        comp[:, pl.ds(base + 128, SLOTS)] = x[:, 128:]
        return offset + count[0, where[0]]

    total = owners(pack)
    blocks = (total + BLOCK - 1) // BLOCK
    centre = centre_ref[:, 0:1]
    row = lax.broadcasted_iota(jnp.int32, (8, 1), 0)
    scale = jnp.where(row < 3, POS_SCALE, VEL_SCALE)

    def columns(i):
        return pl.ds(pl.multiple_of(i * BLOCK, BLOCK), BLOCK)

    def make_factor(i):
        t = (comp[:, columns(i)] - centre) * scale
        square = t[0:1] * t[0:1] + t[1:2] * t[1:2] + t[2:3] * t[2:3] + soften * POS_SCALE**2
        product = t[0:1] * t[3:4] + t[1:2] * t[4:5] + t[2:3] * t[5:6]
        a, b, c = split3(jnp.concatenate([t[0:6], square, product], axis=0))
        ones = jnp.ones((8, BLOCK), f32)
        fill = jnp.zeros((200, BLOCK), f32)
        factor[...] = jnp.concatenate([a, a, b, b, a, c, ones, fill], axis=0).astype(bf16)

    def combine(i):
        sw = raw[0:8] + (raw[8:16] + (raw[32:40] + raw[40:48]))
        sb = raw[16:24] + (raw[24:32] + (raw[64:72] + raw[72:80]))
        t = comp[:, columns(i)] - centre
        rw = (sw - t * sw[6:7]) * (1.0 / W_SCALE)
        rb = pltpu.roll(sb - t * sb[6:7], 3, 0)
        sums[:, columns(i)] = rw - jnp.where((row >= 3) & (row < 6), 3.0 * rb, 0.0)

    def products(acc_q, acc_r, acc_w, acc_b, acc_lw, acc_lb):
        def stage_one(c, buffer, load):
            part = slice(c * CHUNK, (c + 1) * CHUNK)
            blank = jnp.zeros((CHUNK, 128), bf16)
            pltpu.matmul_acc_lhs(
                acc_q[buffer], jnp.concatenate([hq[part], blank], axis=1), load_staged_rhs=load
            )
            pltpu.matmul_acc_lhs(acc_r[buffer], jnp.concatenate([hr[part], blank], axis=1))

        def stage_factor(i):
            make_factor(i)
            pltpu.matmul_push_rhs(factor[...], 0, 0)

        def pop_sums():
            raw[0:16] = pltpu.matmul_pop(acc_w)
            raw[16:32] = pltpu.matmul_pop(acc_b)
            raw[32:64] = pltpu.matmul_pop(acc_lw)
            raw[64:96] = pltpu.matmul_pop(acc_lb)

        chunks = STARS // CHUNK

        def block(i, carry):
            for c in range(chunks):
                if c == chunks - 1:
                    stage_factor(i + 1)
                    stage_one(0, 0, 0)
                else:
                    stage_one(c + 1, (c + 1) % 2, None)
                q = pltpu.matmul_pop(acc_q[c % 2])
                rv = pltpu.matmul_pop(acc_r[c % 2])
                inv = lax.rsqrt(q)
                inv2 = inv * inv
                w = inv2 * inv
                b = w * inv2 * rv
                w_high = w.astype(bf16)
                b_high = b.astype(bf16)
                w_low = (w - w_high.astype(f32)).astype(f8)
                b_low = (b - b_high.astype(f32)).astype(f8)
                if c == 0:
                    pop_sums()
                part = slice(c * CHUNK, (c + 1) * CHUNK)
                pltpu.matmul_push_rhs(w_high, 0, 1)
                pltpu.matmul_acc_lhs(acc_w, fw[:, part], load_staged_rhs=0)
                pltpu.matmul_push_rhs(b_high, 1, 1)
                pltpu.matmul_acc_lhs(acc_b, fw[:, part], load_staged_rhs=1)
                pltpu.matmul_push_rhs(w_low, 0, 1)
                pltpu.matmul_acc_lhs(acc_lw, fl[:, part], load_staged_rhs=0)
                pltpu.matmul_push_rhs(b_low, 1, 1)
                pltpu.matmul_acc_lhs(acc_lb, fl[:, part], load_staged_rhs=1)
                if c == 0:
                    combine(jnp.maximum(i - 1, 0))
            return carry

        pop_sums()
        for k in range(2):
            pltpu.matmul_pop(acc_q[k])
            pltpu.matmul_pop(acc_r[k])
        stage_factor(0)
        stage_one(0, 0, 0)
        lax.fori_loop(0, blocks, block, 0)
        pltpu.matmul_pop(acc_q[0])
        pltpu.matmul_pop(acc_r[0])
        pop_sums()
        combine(jnp.maximum(blocks - 1, 0))

    pl.run_scoped(
        products,
        [pltpu.ACC(0)((CHUNK, BLOCK), f32)] * 2,
        [pltpu.ACC(0)((CHUNK, BLOCK), f32)] * 2,
        *[pltpu.ACC(1)((16, BLOCK), f32)] * 2,
        *[pltpu.ACC(1)((32, BLOCK), f32)] * 2,
    )

    def unpack(where, offset):
        shift = offset % 128
        base = pl.multiple_of(offset - shift, 128)
        x = sums[:, pl.ds(base, SLOTS + 128)]
        x = pltpu.roll(x, (SLOTS + 128) - shift, 1)
        for p in range(PAIRS):
            outs[p][where[p]] = fold(x[2 * p:2 * p + 2, 0:SLOTS])
        return offset + count[0, where[0]]

    owners(unpack)


def pair_scratch():
    return [
        pltpu.VMEM((8, ROOM), f32),
        pltpu.VMEM((8, ROOM), f32),
        pltpu.VMEM((256, BLOCK), bf16),
        pltpu.VMEM((96, BLOCK), f32),
        pltpu.VMEM((8, 128), jnp.int32),
        pltpu.SMEM((8, 128), jnp.int32),
        pltpu.SemaphoreType.DMA,
    ]


def reduce_kernel(
    part0, part1, part2, start_ref, count_ref, out_ref,
    got_core, got_1, got_2, got_3, sum_1, sum_2, send_sem, recv_sem,
):
    part = (part0, part1, part2)
    barrier = greet()
    me, core = place()
    started = []

    def send(p, phase, k, src, dst, target):
        c = pltpu.make_async_remote_copy(
            src_ref=src, dst_ref=dst, send_sem=send_sem.at[p, phase, k],
            recv_sem=recv_sem.at[p, phase, k], device_id=target, device_id_type=MESH,
        )
        c.start()
        started.append(c)
        return c

    def third(p, d):
        return (me[AXES[p][2]] + d) % 4

    pl.semaphore_wait(barrier, 10)
    over = [[None] * PAIRS for _ in range(5)]
    for d in (1, 2, 3, 4):
        for p in range(PAIRS):
            over[d][p] = send(
                p, 0, d - 1, part[p].at[1 - core, third(p, d)], got_core[p].at[d - 1],
                device(me, 1 - core),
            )
    first = [[] for _ in range(PAIRS)]
    for d in (1, 2, 3, 4):
        for p in range(PAIRS):
            over[d][p].wait_recv()
            sum_1[p][d - 1] = part[p][core, third(p, d)] + got_core[p][d - 1]
            if d < 4:
                axis = AXES[p][2]
                first[p].append(send(
                    p, 1, d - 1, sum_1[p].at[d - 1], got_1[p].at[d - 1],
                    along(me, core, axis, d),
                ))
    second = [[] for _ in range(PAIRS)]
    for p in range(PAIRS):
        axis = AXES[p][0]
        for c in first[p]:
            c.wait_recv()
        sum_1[p][3] = sum_1[p][3] + (got_1[p][0] + got_1[p][1] + got_1[p][2])
        for d in (1, 2, 3):
            line = pl.ds((me[axis] + d) % 4 * 4, 4)
            second[p].append(send(
                p, 2, d - 1, sum_1[p].at[3, line], got_2[p].at[d - 1], along(me, core, axis, d)
            ))
    last = [[] for _ in range(PAIRS)]
    for p in range(PAIRS):
        axis = AXES[p][1]
        for c in second[p]:
            c.wait_recv()
        own = sum_1[p][3, pl.ds(me[AXES[p][0]] * 4, 4)]
        sum_2[p][...] = own + (got_2[p][0] + got_2[p][1] + got_2[p][2])
        for d in (1, 2, 3):
            last[p].append(send(
                p, 3, d - 1, sum_2[p].at[(me[axis] + d) % 4], got_3[p].at[d - 1],
                along(me, core, axis, d),
            ))
    blocks = []
    for p in range(PAIRS):
        for c in last[p]:
            c.wait_recv()
        blocks.append(sum_2[p][me[AXES[p][1]]] + (got_3[p][0] + got_3[p][1] + got_3[p][2]))

    total = unfold(blocks) * (1.0 / (STARS * OWNERS))
    start = start_ref[...]
    step = start[12:13]
    acc0, jerk0 = start[6:9], start[9:12]
    acc1, jerk1 = total[0:3], total[3:6]
    vel1 = start[3:6] + (acc0 + acc1) * step / 2.0 + (jerk0 - jerk1) * step * step / 12.0
    pos1 = start[0:3] + (start[3:6] + vel1) * step / 2.0 + (acc0 - acc1) * step * step / 12.0
    state = jnp.concatenate([pos1, vel1, acc1, jerk1], axis=0)
    live = lax.broadcasted_iota(jnp.int32, (12, SLOTS), 1) < count_ref[0]
    out_ref[...] = jnp.where(live, state, 0.0)
    for c in started:
        c.wait_send()


def shards(
    positions, velocities, old_acc, old_jerk, masses, elapsed, levels, active_index, active_count
):
    def lines(a):
        return a.reshape(STARS // 128, 128)

    def near(a):
        return pltpu.with_memory_space_constraint(a, pltpu.VMEM)

    def params(collective_id=None):
        extra = {} if collective_id is None else {
            "collective_id": collective_id, "has_side_effects": True
        }
        return pltpu.CompilerParams(vmem_limit_bytes=VMEM_LIMIT, **extra)

    *every, start, hq, hr, fw, fl, centre = pl.pallas_call(
        gather_kernel,
        out_shape=[pltpu.VMEM(PLACES, f32)] * PAIRS + [
            pltpu.VMEM((16, SLOTS), f32),
            pltpu.VMEM((STARS, 128), bf16),
            pltpu.VMEM((STARS, 128), bf16),
            pltpu.VMEM((16, STARS), bf16),
            pltpu.VMEM((32, STARS), f8),
            pltpu.VMEM((8, 128), f32),
        ],
        in_specs=[vmem()] * 8 + [smem()],
        out_specs=[vmem()] * (PAIRS + 6),
        scratch_shapes=[
            pltpu.VMEM((16, STARS), f32),
            pltpu.SemaphoreType.DMA((PAIRS, 4, 4)),
            pltpu.SemaphoreType.DMA((PAIRS, 4, 4)),
        ],
        compiler_params=params(0),
        name="predict_gather",
    )(
        *[
            pltpu.with_memory_space_constraint(a, pltpu.HBM)
            for a in (positions, velocities, old_acc, old_jerk, lines(masses), lines(elapsed),
                      lines(levels), active_index)
        ],
        active_count,
    )
    parts = pl.pallas_call(
        pair_kernel,
        out_shape=[pltpu.VMEM((OWNERS, 8, 128), f32)] * PAIRS,
        in_specs=[vmem()] * 8,
        out_specs=[vmem()] * PAIRS,
        scratch_shapes=pair_scratch(),
        compiler_params=params(),
        name="pair_sums",
    )(*[near(e.reshape(OWNERS, 8, 128)) for e in every], near(hq), near(hr), near(fw), near(fl), near(centre))

    def buffers(*shape):
        return [pltpu.VMEM(shape + (8, 128), f32)] * PAIRS

    return pl.pallas_call(
        reduce_kernel,
        out_shape=jax.ShapeDtypeStruct((12, SLOTS), f32),
        in_specs=[vmem()] * (PAIRS + 1) + [smem()],
        out_specs=vmem(),
        scratch_shapes=[
            buffers(4, 16),
            buffers(3, 16),
            buffers(3, 4),
            buffers(3),
            buffers(4, 16),
            buffers(4),
            pltpu.SemaphoreType.DMA((PAIRS, 4, 4)),
            pltpu.SemaphoreType.DMA((PAIRS, 4, 4)),
        ],
        compiler_params=params(1),
        name="reduce_correct",
    )(*[near(p.reshape(PLACES)) for p in parts], near(start), active_count)


def solution(mesh):
    every = ("ia", "ja")
    in_specs = (
        P(None, every), P(None, every), P(None, every), P(None, every),
        P(every), P(every), P(every), P(every, None), P(every),
    )
    return jax.shard_map(
        shards, mesh=mesh, in_specs=in_specs, out_specs=P(None, every), check_vma=False
    )
```

```python
import jax
import jax.numpy as jnp
from jax import lax
from jax.experimental import pallas as pl
from jax.experimental.pallas import tpu as pltpu
from jax.sharding import PartitionSpec as P

MESH = pl.DeviceIdType.MESH
soften = 0.01
f32 = jnp.float32
bf16 = jnp.bfloat16
f8 = jnp.float8_e4m3fn

STARS = 1536
SLOTS = 512
SOURCES = 2 * STARS
HALF = SLOTS // 2
OWNERS = 128
BLOCK = 256
CHUNK = 256
TURN = 2
ROOM = OWNERS * HALF + HALF + 128
VMEM_LIMIT = 24 * 2**20
PAIRS = 3
AXES = ("xyz", "yzx", "zxy")
PLACES = (4, 16, 2, 4, 128)
POS_SCALE = 2.0**-2
VEL_SCALE = 2.0**-8
W_SCALE = 2.0**6


def vmem():
    return pl.BlockSpec(memory_space=pltpu.VMEM)


def smem():
    return pl.BlockSpec(memory_space=pltpu.SMEM)


def split3(x):
    a = x.astype(bf16).astype(f32)
    rest = x - a
    b = rest.astype(bf16).astype(f32)
    return a, b, rest - b


def place():
    ia, ja = lax.axis_index("ia"), lax.axis_index("ja")
    return {"z": ia // 2, "x": (ia % 2) * 2 + (ja // 2) % 2, "y": ja // 4}, ja % 2


def device(at, core):
    return (at["z"] * 2 + at["x"] // 2, at["y"] * 4 + (at["x"] % 2) * 2 + core)


def along(me, core, axis, d):
    return device({**me, axis: (me[axis] + d) % 4}, core)


def greet():
    me, core = place()
    barrier = pltpu.get_barrier_semaphore()
    peers = [along(me, c, axis, d) for c in (core, 1 - core) for axis in "xyz" for d in (1, 2, 3)]
    for peer in [device(me, 1 - core)] + peers:
        pl.semaphore_signal(barrier, inc=1, device_id=peer, device_id_type=MESH)
    return barrier, 1 + len(peers)


def predict(d, step):
    tau_sq = 0.5 * step * step
    tau_cube = step * step * step / 6.0
    pos = d[0:3] + step * d[3:6] + tau_sq * d[6:9] + tau_cube * d[9:12]
    vel = d[3:6] + step * d[6:9] + tau_sq * d[9:12]
    return pos, vel


def flat(ref):
    return jnp.concatenate([ref[i:i + 1, :] for i in range(STARS // 128)], axis=1)


def fold(rows):
    return jnp.concatenate([rows[:, 128 * t:128 * (t + 1)] for t in range(2)], axis=0)


def unfold(blocks):
    return jnp.concatenate(
        [jnp.concatenate([b[2 * t:2 * t + 2] for b in blocks], axis=0) for t in range(2)], axis=1
    )


def slot_of(shape, axis):
    j = lax.broadcasted_iota(jnp.int32, shape, axis)
    return jnp.where(j < HALF, 2 * j, 2 * j - (SLOTS - 1))


def reorder(rows, back):
    own = lax.broadcasted_iota(jnp.int32, (SLOTS, SLOTS), 1 if back else 0)
    move = (own == slot_of((SLOTS, SLOTS), 0 if back else 1)).astype(f32).astype(bf16)
    n = rows.shape[0]
    parts = jnp.concatenate(split3(rows), axis=0).astype(bf16)
    out = jnp.dot(parts, move, preferred_element_type=f32)
    return (out[0:n] + out[n:2 * n]) + out[2 * n:3 * n]


def gather_kernel(
    pos_ref, vel_ref, acc_ref, jerk_ref, mass_ref, elapsed_ref, levels_ref, index_ref, count_ref,
    all0, all1, all2, start_ref, hq_ref, hr_ref, fw_ref, f8_ref, centre_ref,
    state, src_ref, other, send_sem, recv_sem,
):
    every = (all0, all1, all2)
    barrier, greeted = greet()
    me, core = place()
    started = []

    def send(p, k, src, dst, target):
        c = pltpu.make_async_remote_copy(
            src_ref=src, dst_ref=dst, send_sem=send_sem.at[p, k],
            recv_sem=recv_sem.at[p, k], device_id=target, device_id_type=MESH,
        )
        c.start()
        started.append(c)
        return c

    state[...] = jnp.zeros_like(state)
    state[0:3] = pos_ref[...]
    state[3:6] = vel_ref[...]
    state[6:9] = acc_ref[...]
    state[9:12] = jerk_ref[...]
    levels = flat(levels_ref)
    step = jnp.where(
        levels == 0, 0.5, jnp.where(levels == 1, 0.25, jnp.where(levels == 2, 0.125, 0.0625))
    ).astype(f32)
    state[12:13] = step

    pick = (lax.broadcasted_iota(jnp.int32, (STARS, SLOTS), 0) == index_ref[...]).astype(f32)
    pick = pick.astype(bf16)
    parts = jnp.concatenate(split3(state[...]), axis=0).astype(bf16)
    rows = jnp.dot(parts, pick, preferred_element_type=f32)
    start = (rows[0:16] + rows[16:32]) + rows[32:48]
    start_ref[...] = start
    target = jnp.concatenate(predict(start, start[12:13]), axis=0)
    live = lax.broadcasted_iota(jnp.int32, (8, SLOTS), 1) < count_ref[0]
    target = reorder(jnp.concatenate([target, jnp.zeros((2, SLOTS), f32)], axis=0), False)
    marks = slot_of((8, SLOTS), 1) < count_ref[0]
    pairs = (jnp.where(marks[0:2], target[0:2], 1e30), target[2:4], target[4:6])
    for p in range(PAIRS):
        one, two, three = (me[axis] for axis in AXES[p])
        even, odd = fold(pairs[p][:, 0:HALF]), fold(pairs[p][:, HALF:])
        every[p][three, one * 4 + two, core] = jnp.where(core == 0, even, odd)
        other[p] = jnp.where(core == 0, odd, even)

    pl.semaphore_wait(barrier, greeted)

    flight = [[] for _ in range(PAIRS)]

    def begin(phase):
        for p in range(PAIRS):
            one, two, three = (me[axis] for axis in AXES[p])
            block = every[p].at[three]
            if phase == 0:
                block = block.at[one * 4 + two, core]
            elif phase == 1:
                block = block.at[pl.ds(one * 4, 4)]
            axis = AXES[p][(1, 0, 2)[phase]]
            flight[p] = [
                send(p, 3 * phase + d - 1, block, block, along(me, core, axis, d))
                for d in (1, 2, 3)
            ]
            if phase == 0:
                flight[p] += [
                    send(p, 9 + d, other.at[p], block, along(me, 1 - core, axis, d))
                    for d in range(4)
                ]

    def finish():
        for p in range(PAIRS):
            for c in flight[p]:
                c.wait_recv()

    begin(0)
    chosen = lax.dot_general(
        live.astype(f32).astype(bf16), pick, (((1,), (1,)), ((), ())),
        preferred_element_type=f32,
    )[0:1]
    interval = jnp.where(chosen > 0.5, step, flat(elapsed_ref))
    src = jnp.concatenate(predict(state[...], interval), axis=0)
    mass = flat(mass_ref)
    src_ref[core] = jnp.concatenate([src, mass, jnp.zeros_like(mass)], axis=0)
    share = send(0, 13, src_ref.at[core], src_ref.at[core], device(me, 1 - core))
    finish()
    begin(1)
    share.wait_recv()

    src = jnp.concatenate([src_ref[0], src_ref[1]], axis=1)
    mass = src[6:7]
    src = src[0:6]
    centre = jnp.sum(src, axis=1, keepdims=True) * (1.0 / SOURCES)
    centre = jnp.floor(centre * 64.0 + 0.5) * (1.0 / 64.0)
    src = src - centre
    centre = jnp.concatenate([centre, jnp.zeros((2, 1), f32)], axis=0)
    centre_ref[...] = jnp.broadcast_to(centre, (8, 128))
    zero = jnp.zeros((1, SOURCES), f32)
    weights = jnp.concatenate([src, zero + 1.0, zero], axis=0) * mass
    pos, vel = src[0:3] * POS_SCALE, src[3:6] * VEL_SCALE
    row = lax.broadcasted_iota(jnp.int32, (8, 1), 0)

    def factors(own, square, unit):
        a, b, c = split3(jnp.concatenate([own, zero, zero], axis=0))
        a = a + (row == unit).astype(f32)
        s = jnp.concatenate(split3(square) + (zero,) * 5, axis=0)
        fill = jnp.zeros((72, SOURCES), f32)
        return jnp.concatenate([a, b, a, b, c, a, s, fill], axis=0).T.astype(bf16)

    square = pos[0:1] * pos[0:1] + pos[1:2] * pos[1:2] + pos[2:3] * pos[2:3]
    hq_ref[...] = factors(jnp.concatenate([pos * -2.0, zero, zero, zero], axis=0), square, 6)
    finish()
    begin(2)
    product = pos[0:1] * vel[0:1] + pos[1:2] * vel[1:2] + pos[2:3] * vel[2:3]
    hr_ref[...] = factors(jnp.concatenate([-vel, -pos], axis=0), product, 7)
    fill = jnp.zeros((8, SOURCES), f32)
    fw_ref[...] = jnp.concatenate(split3(weights)[0:2], axis=0).astype(bf16)
    high = weights.astype(f8).astype(f32)
    f8_ref[...] = jnp.concatenate([high, weights - high, fill, fill], axis=0).astype(f8)

    finish()
    for c in started:
        c.wait_send()


def pair_kernel(
    all0, all1, all2, hq, hr, fw, fl, centre_ref,
    out0, out1, out2,
    comp, sums, factor, raw, counts, count, sem,
):
    outs = (out0, out1, out2)
    marked = jnp.where(all0[...] < 1e29, 0.5, 0.0)
    counted = jnp.sum(jnp.sum(marked, axis=1), axis=1, keepdims=True)
    counted = jnp.broadcast_to(counted, (OWNERS, 128)).T[0:8]
    counts[...] = counted.astype(jnp.int32)
    copy = pltpu.make_async_copy(counts, count, sem)
    copy.start()
    copy.wait()

    lane = lax.broadcasted_iota(jnp.int32, (8, 128), 1)
    blank = jnp.zeros((2, HALF), f32)

    def owners(step):
        def some(g, offset):
            core, z = g % 2, g // 2
            for x in range(4):
                for y in range(4):
                    at = {"x": x, "y": y, "z": z}
                    where = [
                        (at[three] * 16 + at[one] * 4 + at[two]) * 2 + core
                        for one, two, three in AXES
                    ]
                    offset = step(where, offset)
            return offset

        return lax.fori_loop(0, 8, some, jnp.int32(0))

    def pack(where, offset):
        shift = offset % 128
        base = pl.multiple_of(offset - shift, 128)
        x = unfold([ref[k] for ref, k in zip((all0, all1, all2), where)])
        x = jnp.concatenate([x, blank], axis=0)
        x = jnp.concatenate([x, jnp.zeros((8, 128), f32)], axis=1)
        x = pltpu.roll(x, shift, 1)
        first = pl.ds(base, 128)
        comp[:, first] = jnp.where(lane < shift, comp[:, first], x[:, 0:128])
        comp[:, pl.ds(base + 128, HALF)] = x[:, 128:]
        return offset + count[0, where[0]]

    total = owners(pack)
    blocks = (total + BLOCK - 1) // BLOCK
    centre = centre_ref[:, 0:1]
    row = lax.broadcasted_iota(jnp.int32, (8, 1), 0)
    scale = jnp.where(row < 3, POS_SCALE, VEL_SCALE)

    def columns(i):
        return pl.ds(pl.multiple_of(i * BLOCK, BLOCK), BLOCK)

    def make_factor(i):
        t = (comp[:, columns(i)] - centre) * scale
        square = t[0:1] * t[0:1] + t[1:2] * t[1:2] + t[2:3] * t[2:3] + soften * POS_SCALE**2
        product = t[0:1] * t[3:4] + t[1:2] * t[4:5] + t[2:3] * t[5:6]
        a, b, c = split3(jnp.concatenate([t[0:6], square, product], axis=0))
        ones = jnp.ones((8, BLOCK), f32)
        fill = jnp.zeros((200, BLOCK), f32)
        factor[...] = jnp.concatenate([a, a, b, b, a, c, ones, fill], axis=0).astype(bf16)

    def combine(i):
        sw = raw[0:8] + (raw[8:16] + (raw[32:40] + raw[40:48]))
        sb = raw[16:24] + (raw[24:32] + (raw[64:72] + raw[72:80]))
        t = comp[:, columns(i)] - centre
        rw = (sw - t * sw[6:7]) * (1.0 / W_SCALE)
        rb = pltpu.roll(sb - t * sb[6:7], 3, 0)
        sums[:, columns(i)] = rw - jnp.where((row >= 3) & (row < 6), 3.0 * rb, 0.0)

    def products(acc_q, acc_r, acc_w, acc_b, acc_lw, acc_lb):
        def stage_one(c, buffer, load):
            part = slice(c * CHUNK, (c + 1) * CHUNK)
            blank = jnp.zeros((CHUNK, 128), bf16)
            pltpu.matmul_acc_lhs(
                acc_q[buffer], jnp.concatenate([hq[part], blank], axis=1), load_staged_rhs=load
            )
            pltpu.matmul_acc_lhs(acc_r[buffer], jnp.concatenate([hr[part], blank], axis=1))

        def stage_factor(i):
            make_factor(i)
            pltpu.matmul_push_rhs(factor[...], 0, 0)

        def pop_sums():
            raw[0:16] = pltpu.matmul_pop(acc_w)
            raw[16:32] = pltpu.matmul_pop(acc_b)
            raw[32:64] = pltpu.matmul_pop(acc_lw)
            raw[64:96] = pltpu.matmul_pop(acc_lb)

        chunks = SOURCES // CHUNK

        def block(i):
            for c in range(chunks):
                if c == chunks - 1:
                    stage_factor(i + 1)
                    stage_one(0, 0, 0)
                else:
                    stage_one(c + 1, (c + 1) % 2, None)
                q = pltpu.matmul_pop(acc_q[c % 2])
                rv = pltpu.matmul_pop(acc_r[c % 2])
                inv = lax.rsqrt(q)
                inv2 = inv * inv
                w = inv2 * inv
                b = w * inv2 * rv
                w_high = w.astype(bf16)
                b_high = b.astype(bf16)
                w_low = (w - w_high.astype(f32)).astype(f8)
                b_low = (b - b_high.astype(f32)).astype(f8)
                if c == 0:
                    pop_sums()
                part = slice(c * CHUNK, (c + 1) * CHUNK)
                pltpu.matmul_push_rhs(w_high, 0, 1)
                pltpu.matmul_acc_lhs(acc_w, fw[:, part], load_staged_rhs=0)
                pltpu.matmul_push_rhs(b_high, 1, 1)
                pltpu.matmul_acc_lhs(acc_b, fw[:, part], load_staged_rhs=1)
                pltpu.matmul_push_rhs(w_low, 0, 1)
                pltpu.matmul_acc_lhs(acc_lw, fl[:, part], load_staged_rhs=0)
                pltpu.matmul_push_rhs(b_low, 1, 1)
                pltpu.matmul_acc_lhs(acc_lb, fl[:, part], load_staged_rhs=1)
                if c == 0:
                    combine(jnp.maximum(i - 1, 0))

        def several(j, carry):
            for k in range(TURN):
                block(j * TURN + k)
            return carry

        pop_sums()
        for k in range(2):
            pltpu.matmul_pop(acc_q[k])
            pltpu.matmul_pop(acc_r[k])
        stage_factor(0)
        stage_one(0, 0, 0)
        lax.fori_loop(0, blocks // TURN, several, 0)

        def single(i, carry):
            block(i)
            return carry

        lax.fori_loop(blocks // TURN * TURN, blocks, single, 0)
        pltpu.matmul_pop(acc_q[0])
        pltpu.matmul_pop(acc_r[0])
        pop_sums()
        combine(jnp.maximum(blocks - 1, 0))

    pl.run_scoped(
        products,
        [pltpu.ACC(0)((CHUNK, BLOCK), f32)] * 2,
        [pltpu.ACC(0)((CHUNK, BLOCK), f32)] * 2,
        *[pltpu.ACC(1)((16, BLOCK), f32)] * 2,
        *[pltpu.ACC(1)((32, BLOCK), f32)] * 2,
    )

    def unpack(where, offset):
        shift = offset % 128
        base = pl.multiple_of(offset - shift, 128)
        x = sums[:, pl.ds(base, HALF + 128)]
        x = pltpu.roll(x, (HALF + 128) - shift, 1)
        for p in range(PAIRS):
            outs[p][where[p]] = fold(x[2 * p:2 * p + 2, 0:HALF])
        return offset + count[0, where[0]]

    owners(unpack)


def pair_scratch():
    return [
        pltpu.VMEM((8, ROOM), f32),
        pltpu.VMEM((8, ROOM), f32),
        pltpu.VMEM((256, BLOCK), bf16),
        pltpu.VMEM((96, BLOCK), f32),
        pltpu.VMEM((8, 128), jnp.int32),
        pltpu.SMEM((8, 128), jnp.int32),
        pltpu.SemaphoreType.DMA,
    ]


def reduce_kernel(
    part0, part1, part2, start_ref, count_ref, out_ref,
    got_1, got_2, got_3, got_other, sum_1, sum_2, send_sem, recv_sem,
):
    part = (part0, part1, part2)
    barrier, greeted = greet()
    me, core = place()
    started = []

    def send(p, k, src, dst, target):
        c = pltpu.make_async_remote_copy(
            src_ref=src, dst_ref=dst, send_sem=send_sem.at[p, k],
            recv_sem=recv_sem.at[p, k], device_id=target, device_id_type=MESH,
        )
        c.start()
        started.append(c)
        return c

    pl.semaphore_wait(barrier, greeted)
    first = [[] for _ in range(PAIRS)]
    for p in range(PAIRS):
        axis = AXES[p][2]
        for d in (1, 2, 3):
            first[p].append(send(
                p, d - 1, part[p].at[(me[axis] + d) % 4], got_1[p].at[d - 1],
                along(me, core, axis, d),
            ))
    second = [[] for _ in range(PAIRS)]
    for p in range(PAIRS):
        axis = AXES[p][0]
        for c in first[p]:
            c.wait_recv()
        own = part[p][me[AXES[p][2]]]
        sum_1[p][...] = own + (got_1[p][0] + got_1[p][1] + got_1[p][2])
        for d in (1, 2, 3):
            line = pl.ds((me[axis] + d) % 4 * 4, 4)
            second[p].append(send(
                p, 2 + d, sum_1[p].at[line], got_2[p].at[d - 1], along(me, core, axis, d)
            ))
    last = [[] for _ in range(PAIRS)]
    for p in range(PAIRS):
        axis = AXES[p][1]
        for c in second[p]:
            c.wait_recv()
        own = sum_1[p][pl.ds(me[AXES[p][0]] * 4, 4)]
        sum_2[p][...] = own + (got_2[p][0] + got_2[p][1] + got_2[p][2])
        for d in (1, 2, 3):
            last[p].append(send(
                p, 5 + d, sum_2[p].at[(me[axis] + d) % 4, core], got_3[p].at[d - 1],
                along(me, core, axis, d),
            ))
        for d in range(4):
            last[p].append(send(
                p, 9 + d, sum_2[p].at[(me[axis] + d) % 4, 1 - core], got_other[p].at[d],
                along(me, 1 - core, axis, d),
            ))
    mine, others = [], []
    for p in range(PAIRS):
        for c in last[p]:
            c.wait_recv()
        own = sum_2[p][me[AXES[p][1]], core]
        mine.append(own + (got_3[p][0] + got_3[p][1] + got_3[p][2]))
        others.append(
            (got_other[p][0] + got_other[p][1]) + (got_other[p][2] + got_other[p][3])
        )
    mine, others = unfold(mine), unfold(others)
    halves = [jnp.where(core == 0, mine, others), jnp.where(core == 0, others, mine)]
    total = jnp.concatenate(
        [jnp.concatenate(halves, axis=1), jnp.zeros((2, SLOTS), f32)], axis=0
    )
    total = jnp.where(slot_of((8, SLOTS), 1) < count_ref[0], total, 0.0)
    total = reorder(total, True) * (1.0 / (STARS * OWNERS))
    start = start_ref[...]
    step = start[12:13]
    acc0, jerk0 = start[6:9], start[9:12]
    acc1, jerk1 = total[0:3], total[3:6]
    vel1 = start[3:6] + (acc0 + acc1) * step / 2.0 + (jerk0 - jerk1) * step * step / 12.0
    pos1 = start[0:3] + (start[3:6] + vel1) * step / 2.0 + (acc0 - acc1) * step * step / 12.0
    state = jnp.concatenate([pos1, vel1, acc1, jerk1], axis=0)
    live = lax.broadcasted_iota(jnp.int32, (12, SLOTS), 1) < count_ref[0]
    out_ref[...] = jnp.where(live, state, 0.0)
    for c in started:
        c.wait_send()


def shards(
    positions, velocities, old_acc, old_jerk, masses, elapsed, levels, active_index, active_count
):
    def lines(a):
        return a.reshape(STARS // 128, 128)

    def near(a):
        return pltpu.with_memory_space_constraint(a, pltpu.VMEM)

    def params(collective_id=None):
        extra = {} if collective_id is None else {
            "collective_id": collective_id, "has_side_effects": True
        }
        return pltpu.CompilerParams(vmem_limit_bytes=VMEM_LIMIT, **extra)

    *every, start, hq, hr, fw, fl, centre = pl.pallas_call(
        gather_kernel,
        out_shape=[pltpu.VMEM(PLACES, f32)] * PAIRS + [
            pltpu.VMEM((16, SLOTS), f32),
            pltpu.VMEM((SOURCES, 128), bf16),
            pltpu.VMEM((SOURCES, 128), bf16),
            pltpu.VMEM((16, SOURCES), bf16),
            pltpu.VMEM((32, SOURCES), f8),
            pltpu.VMEM((8, 128), f32),
        ],
        in_specs=[vmem()] * 8 + [smem()],
        out_specs=[vmem()] * (PAIRS + 6),
        scratch_shapes=[
            pltpu.VMEM((16, STARS), f32),
            pltpu.VMEM((2, 8, STARS), f32),
            pltpu.VMEM((PAIRS, 4, 128), f32),
            pltpu.SemaphoreType.DMA((PAIRS, 14)),
            pltpu.SemaphoreType.DMA((PAIRS, 14)),
        ],
        compiler_params=params(0),
        name="predict_gather",
    )(
        *[
            pltpu.with_memory_space_constraint(a, pltpu.HBM)
            for a in (positions, velocities, old_acc, old_jerk, lines(masses), lines(elapsed),
                      lines(levels), active_index)
        ],
        active_count,
    )
    parts = pl.pallas_call(
        pair_kernel,
        out_shape=[pltpu.VMEM((OWNERS, 4, 128), f32)] * PAIRS,
        in_specs=[vmem()] * 8,
        out_specs=[vmem()] * PAIRS,
        scratch_shapes=pair_scratch(),
        compiler_params=params(),
        name="pair_sums",
    )(*[near(e.reshape(OWNERS, 4, 128)) for e in every], near(hq), near(hr), near(fw), near(fl), near(centre))

    def buffers(*shape):
        return [pltpu.VMEM(shape + (4, 128), f32)] * PAIRS

    return pl.pallas_call(
        reduce_kernel,
        out_shape=jax.ShapeDtypeStruct((12, SLOTS), f32),
        in_specs=[vmem()] * (PAIRS + 1) + [smem()],
        out_specs=vmem(),
        scratch_shapes=[
            buffers(3, 16, 2),
            buffers(3, 4, 2),
            buffers(3),
            buffers(4),
            buffers(16, 2),
            buffers(4, 2),
            pltpu.SemaphoreType.DMA((PAIRS, 14)),
            pltpu.SemaphoreType.DMA((PAIRS, 14)),
        ],
        compiler_params=params(1),
        name="reduce_correct",
    )(*[near(p.reshape(PLACES)) for p in parts], near(start), active_count)


def solution(mesh):
    every = ("ia", "ja")
    in_specs = (
        P(None, every), P(None, every), P(None, every), P(None, every),
        P(every), P(every), P(every), P(every, None), P(every),
    )
    return jax.shard_map(
        shards, mesh=mesh, in_specs=in_specs, out_specs=P(None, every), check_vma=False
    )
```

```python
import jax
import jax.numpy as jnp
from jax import lax
from jax.experimental import pallas as pl
from jax.experimental.pallas import tpu as pltpu
from jax.sharding import PartitionSpec as P

MESH = pl.DeviceIdType.MESH
soften = 0.01
f32 = jnp.float32
bf16 = jnp.bfloat16
f8 = jnp.float8_e4m3fn

STARS = 1536
SLOTS = 512
SOURCES = 2 * STARS
HALF = SLOTS // 2
OWNERS = 128
BLOCK = 256
CHUNK = 256
TURN = 2
DIRECT = 32
ROOM = OWNERS * HALF + HALF + 128
VMEM_LIMIT = 24 * 2**20
PAIRS = 3
AXES = ("xyz", "yzx", "zxy")
PLACES = (4, 16, 2, 4, 128)
POS_SCALE = 2.0**-2
VEL_SCALE = 2.0**-8
W_SCALE = 2.0**6


def vmem():
    return pl.BlockSpec(memory_space=pltpu.VMEM)


def smem():
    return pl.BlockSpec(memory_space=pltpu.SMEM)


def split3(x):
    a = x.astype(bf16).astype(f32)
    rest = x - a
    b = rest.astype(bf16).astype(f32)
    return a, b, rest - b


def place():
    ia, ja = lax.axis_index("ia"), lax.axis_index("ja")
    return {"z": ia // 2, "x": (ia % 2) * 2 + (ja // 2) % 2, "y": ja // 4}, ja % 2


def device(at, core):
    return (at["z"] * 2 + at["x"] // 2, at["y"] * 4 + (at["x"] % 2) * 2 + core)


def along(me, core, axis, d):
    return device({**me, axis: (me[axis] + d) % 4}, core)


def greet():
    me, core = place()
    barrier = pltpu.get_barrier_semaphore()
    peers = [along(me, c, axis, d) for c in (core, 1 - core) for axis in "xyz" for d in (1, 2, 3)]
    for peer in [device(me, 1 - core)] + peers:
        pl.semaphore_signal(barrier, inc=1, device_id=peer, device_id_type=MESH)
    return barrier, 1 + len(peers)


def predict(d, step):
    tau_sq = 0.5 * step * step
    tau_cube = step * step * step / 6.0
    pos = d[0:3] + step * d[3:6] + tau_sq * d[6:9] + tau_cube * d[9:12]
    vel = d[3:6] + step * d[6:9] + tau_sq * d[9:12]
    return pos, vel


def flat(ref):
    return jnp.concatenate([ref[i:i + 1, :] for i in range(STARS // 128)], axis=1)


def fold(rows):
    return jnp.concatenate([rows[:, 128 * t:128 * (t + 1)] for t in range(2)], axis=0)


def unfold(blocks):
    return jnp.concatenate(
        [jnp.concatenate([b[2 * t:2 * t + 2] for b in blocks], axis=0) for t in range(2)], axis=1
    )


def slot_of(shape, axis):
    j = lax.broadcasted_iota(jnp.int32, shape, axis)
    return jnp.where(j < HALF, 2 * j, 2 * j - (SLOTS - 1))


def reorder(rows, back):
    own = lax.broadcasted_iota(jnp.int32, (SLOTS, SLOTS), 1 if back else 0)
    move = (own == slot_of((SLOTS, SLOTS), 0 if back else 1)).astype(f32).astype(bf16)
    n = rows.shape[0]
    parts = jnp.concatenate(split3(rows), axis=0).astype(bf16)
    out = jnp.dot(parts, move, preferred_element_type=f32)
    return (out[0:n] + out[n:2 * n]) + out[2 * n:3 * n]


def gather_kernel(
    pos_ref, vel_ref, acc_ref, jerk_ref, mass_ref, elapsed_ref, levels_ref, index_ref, count_ref,
    all0, all1, all2, start_ref, hq_ref, hr_ref, fw_ref, f8_ref, centre_ref, wide_ref,
    state, src_ref, other, send_sem, recv_sem,
):
    every = (all0, all1, all2)
    barrier, greeted = greet()
    me, core = place()
    started = []

    def send(p, k, src, dst, target):
        c = pltpu.make_async_remote_copy(
            src_ref=src, dst_ref=dst, send_sem=send_sem.at[p, k],
            recv_sem=recv_sem.at[p, k], device_id=target, device_id_type=MESH,
        )
        c.start()
        started.append(c)
        return c

    state[...] = jnp.zeros_like(state)
    state[0:3] = pos_ref[...]
    state[3:6] = vel_ref[...]
    state[6:9] = acc_ref[...]
    state[9:12] = jerk_ref[...]
    levels = flat(levels_ref)
    step = jnp.where(
        levels == 0, 0.5, jnp.where(levels == 1, 0.25, jnp.where(levels == 2, 0.125, 0.0625))
    ).astype(f32)
    state[12:13] = step

    pick = (lax.broadcasted_iota(jnp.int32, (STARS, SLOTS), 0) == index_ref[...]).astype(f32)
    pick = pick.astype(bf16)
    parts = jnp.concatenate(split3(state[...]), axis=0).astype(bf16)
    rows = jnp.dot(parts, pick, preferred_element_type=f32)
    start = (rows[0:16] + rows[16:32]) + rows[32:48]
    start_ref[...] = start
    target = jnp.concatenate(predict(start, start[12:13]), axis=0)
    live = lax.broadcasted_iota(jnp.int32, (8, SLOTS), 1) < count_ref[0]
    target = reorder(jnp.concatenate([target, jnp.zeros((2, SLOTS), f32)], axis=0), False)
    marks = slot_of((8, SLOTS), 1) < count_ref[0]
    pairs = (jnp.where(marks[0:2], target[0:2], 1e30), target[2:4], target[4:6])
    for p in range(PAIRS):
        one, two, three = (me[axis] for axis in AXES[p])
        even, odd = fold(pairs[p][:, 0:HALF]), fold(pairs[p][:, HALF:])
        every[p][three, one * 4 + two, core] = jnp.where(core == 0, even, odd)
        other[p] = jnp.where(core == 0, odd, even)

    pl.semaphore_wait(barrier, greeted)

    flight = [[] for _ in range(PAIRS)]

    def begin(phase):
        for p in range(PAIRS):
            one, two, three = (me[axis] for axis in AXES[p])
            block = every[p].at[three]
            if phase == 0:
                block = block.at[one * 4 + two, core]
            elif phase == 1:
                block = block.at[pl.ds(one * 4, 4)]
            axis = AXES[p][(1, 0, 2)[phase]]
            flight[p] = [
                send(p, 3 * phase + d - 1, block, block, along(me, core, axis, d))
                for d in (1, 2, 3)
            ]
            if phase == 0:
                flight[p] += [
                    send(p, 9 + d, other.at[p], block, along(me, 1 - core, axis, d))
                    for d in range(4)
                ]

    def finish():
        for p in range(PAIRS):
            for c in flight[p]:
                c.wait_recv()

    begin(0)
    chosen = lax.dot_general(
        live.astype(f32).astype(bf16), pick, (((1,), (1,)), ((), ())),
        preferred_element_type=f32,
    )[0:1]
    interval = jnp.where(chosen > 0.5, step, flat(elapsed_ref))
    src = jnp.concatenate(predict(state[...], interval), axis=0)
    mass = flat(mass_ref)
    src_ref[core] = jnp.concatenate([src, mass, jnp.zeros_like(mass)], axis=0)
    share = send(0, 13, src_ref.at[core], src_ref.at[core], device(me, 1 - core))
    finish()
    begin(1)
    share.wait_recv()

    src = jnp.concatenate([src_ref[0], src_ref[1]], axis=1)
    mass = src[6:7]
    src = src[0:6]
    centre = jnp.sum(src, axis=1, keepdims=True) * (1.0 / SOURCES)
    centre = jnp.floor(centre * 64.0 + 0.5) * (1.0 / 64.0)
    src = src - centre
    centre = jnp.concatenate([centre, jnp.zeros((2, 1), f32)], axis=0)
    centre_ref[...] = jnp.broadcast_to(centre, (8, 128))
    zero = jnp.zeros((1, SOURCES), f32)
    weights = jnp.concatenate([src, zero + 1.0, zero], axis=0) * mass
    pos, vel = src[0:3] * POS_SCALE, src[3:6] * VEL_SCALE
    row = lax.broadcasted_iota(jnp.int32, (8, 1), 0)

    def factors(own, square, unit):
        a, b, c = split3(jnp.concatenate([own, zero, zero], axis=0))
        a = a + (row == unit).astype(f32)
        s = jnp.concatenate(split3(square) + (zero,) * 5, axis=0)
        fill = jnp.zeros((72, SOURCES), f32)
        return jnp.concatenate([a, b, a, b, c, a, s, fill], axis=0).T.astype(bf16)

    square = pos[0:1] * pos[0:1] + pos[1:2] * pos[1:2] + pos[2:3] * pos[2:3]
    hq_ref[...] = factors(jnp.concatenate([pos * -2.0, zero, zero, zero], axis=0), square, 6)
    finish()
    begin(2)
    product = pos[0:1] * vel[0:1] + pos[1:2] * vel[1:2] + pos[2:3] * vel[2:3]
    hr_ref[...] = factors(jnp.concatenate([-vel, -pos], axis=0), product, 7)
    fill = jnp.zeros((8, SOURCES), f32)
    fw_ref[...] = jnp.concatenate(split3(weights)[0:2], axis=0).astype(bf16)
    high = weights.astype(f8).astype(f32)
    f8_ref[...] = jnp.concatenate([high, weights - high, fill, fill], axis=0).astype(f8)

    columns = jnp.concatenate([pos, jnp.zeros((5, SOURCES), f32)], axis=0)
    for c in range(SOURCES // CHUNK):
        some = columns[:, c * CHUNK:c * CHUNK + 128].T
        for axis in range(3):
            wide_ref[axis, c * DIRECT:(c + 1) * DIRECT] = jnp.broadcast_to(
                some[0:DIRECT, axis:axis + 1], (DIRECT, 128)
            )
    finish()
    for c in started:
        c.wait_send()


def pair_kernel(
    all0, all1, all2, hq, hr, fw, fl, centre_ref, wide_ref,
    out0, out1, out2,
    comp, sums, factor, near_ref, raw, counts, count, sem,
):
    outs = (out0, out1, out2)
    marked = jnp.where(all0[...] < 1e29, 0.5, 0.0)
    counted = jnp.sum(jnp.sum(marked, axis=1), axis=1, keepdims=True)
    counted = jnp.broadcast_to(counted, (OWNERS, 128)).T[0:8]
    counts[...] = counted.astype(jnp.int32)
    copy = pltpu.make_async_copy(counts, count, sem)
    copy.start()
    copy.wait()

    lane = lax.broadcasted_iota(jnp.int32, (8, 128), 1)
    blank = jnp.zeros((2, HALF), f32)

    def owners(step):
        def some(g, offset):
            core, z = g % 2, g // 2
            for x in range(4):
                for y in range(4):
                    at = {"x": x, "y": y, "z": z}
                    where = [
                        (at[three] * 16 + at[one] * 4 + at[two]) * 2 + core
                        for one, two, three in AXES
                    ]
                    offset = step(where, offset)
            return offset

        return lax.fori_loop(0, 8, some, jnp.int32(0))

    def pack(where, offset):
        shift = offset % 128
        base = pl.multiple_of(offset - shift, 128)
        x = unfold([ref[k] for ref, k in zip((all0, all1, all2), where)])
        x = jnp.concatenate([x, blank], axis=0)
        x = jnp.concatenate([x, jnp.zeros((8, 128), f32)], axis=1)
        x = pltpu.roll(x, shift, 1)
        first = pl.ds(base, 128)
        comp[:, first] = jnp.where(lane < shift, comp[:, first], x[:, 0:128])
        comp[:, pl.ds(base + 128, HALF)] = x[:, 128:]
        return offset + count[0, where[0]]

    total = owners(pack)
    blocks = (total + BLOCK - 1) // BLOCK
    centre = centre_ref[:, 0:1]
    row = lax.broadcasted_iota(jnp.int32, (8, 1), 0)
    scale = jnp.where(row < 3, POS_SCALE, VEL_SCALE)

    def columns(i):
        return pl.ds(pl.multiple_of(i * BLOCK, BLOCK), BLOCK)

    def make_factor(i, k):
        t = (comp[:, columns(i)] - centre) * scale
        for axis in range(3):
            near_ref[k, axis] = jnp.broadcast_to(t[axis:axis + 1], (8, BLOCK))
        square = t[0:1] * t[0:1] + t[1:2] * t[1:2] + t[2:3] * t[2:3] + soften * POS_SCALE**2
        product = t[0:1] * t[3:4] + t[1:2] * t[4:5] + t[2:3] * t[5:6]
        a, b, c = split3(jnp.concatenate([t[0:6], square, product], axis=0))
        ones = jnp.ones((8, BLOCK), f32)
        fill = jnp.zeros((200, BLOCK), f32)
        factor[...] = jnp.concatenate([a, a, b, b, a, c, ones, fill], axis=0).astype(bf16)

    def combine(i):
        sw = raw[0:8] + (raw[8:16] + (raw[32:40] + raw[40:48]))
        sb = raw[16:24] + (raw[24:32] + (raw[64:72] + raw[72:80]))
        t = comp[:, columns(i)] - centre
        rw = (sw - t * sw[6:7]) * (1.0 / W_SCALE)
        rb = pltpu.roll(sb - t * sb[6:7], 3, 0)
        sums[:, columns(i)] = rw - jnp.where((row >= 3) & (row < 6), 3.0 * rb, 0.0)

    def products(acc_q, acc_r, acc_w, acc_b, acc_lw, acc_lb):
        def stage_one(c, buffer, load):
            part = slice(c * CHUNK, (c + 1) * CHUNK)
            blank = jnp.zeros((CHUNK, 128), bf16)
            pltpu.matmul_acc_lhs(
                acc_r[buffer], jnp.concatenate([hr[part], blank], axis=1), load_staged_rhs=load
            )
            part = slice(c * CHUNK + DIRECT, (c + 1) * CHUNK)
            pltpu.matmul_acc_lhs(
                acc_q[buffer], jnp.concatenate([hq[part], blank[DIRECT:]], axis=1)
            )

        def direct(c, k):
            total = None
            for axis in range(3):
                wide = wide_ref[axis, c * DIRECT:(c + 1) * DIRECT]
                wide = jnp.concatenate([wide] * (BLOCK // 128), axis=1)
                gap = wide - jnp.concatenate([near_ref[k, axis]] * (DIRECT // 8), axis=0)
                total = gap * gap if total is None else total + gap * gap
            return total + soften * POS_SCALE**2

        def stage_factor(i, k):
            make_factor(i, k)
            pltpu.matmul_push_rhs(factor[...], 0, 0)

        def pop_sums():
            raw[0:16] = pltpu.matmul_pop(acc_w)
            raw[16:32] = pltpu.matmul_pop(acc_b)
            raw[32:64] = pltpu.matmul_pop(acc_lw)
            raw[64:96] = pltpu.matmul_pop(acc_lb)

        chunks = SOURCES // CHUNK

        def block(i, k):
            for c in range(chunks):
                if c == chunks - 1:
                    stage_factor(i + 1, 1 - k)
                    stage_one(0, 0, 0)
                else:
                    stage_one(c + 1, (c + 1) % 2, None)
                q = jnp.concatenate([direct(c, k), pltpu.matmul_pop(acc_q[c % 2])], axis=0)
                rv = pltpu.matmul_pop(acc_r[c % 2])
                inv = lax.rsqrt(q)
                inv2 = inv * inv
                w = inv2 * inv
                b = w * inv2 * rv
                w_high = w.astype(bf16)
                b_high = b.astype(bf16)
                w_low = (w - w_high.astype(f32)).astype(f8)
                b_low = (b - b_high.astype(f32)).astype(f8)
                if c == 0:
                    pop_sums()
                part = slice(c * CHUNK, (c + 1) * CHUNK)
                pltpu.matmul_push_rhs(w_high, 0, 1)
                pltpu.matmul_acc_lhs(acc_w, fw[:, part], load_staged_rhs=0)
                pltpu.matmul_push_rhs(b_high, 1, 1)
                pltpu.matmul_acc_lhs(acc_b, fw[:, part], load_staged_rhs=1)
                pltpu.matmul_push_rhs(w_low, 0, 1)
                pltpu.matmul_acc_lhs(acc_lw, fl[:, part], load_staged_rhs=0)
                pltpu.matmul_push_rhs(b_low, 1, 1)
                pltpu.matmul_acc_lhs(acc_lb, fl[:, part], load_staged_rhs=1)
                if c == 0:
                    combine(jnp.maximum(i - 1, 0))

        def several(j, carry):
            for k in range(TURN):
                block(j * TURN + k, k)
            return carry

        pop_sums()
        for k in range(2):
            pltpu.matmul_pop(acc_q[k])
            pltpu.matmul_pop(acc_r[k])
        stage_factor(0, 0)
        stage_one(0, 0, 0)
        lax.fori_loop(0, blocks // TURN, several, 0)

        def single(i, carry):
            block(i, 0)
            return carry

        lax.fori_loop(blocks // TURN * TURN, blocks, single, 0)
        pltpu.matmul_pop(acc_q[0])
        pltpu.matmul_pop(acc_r[0])
        pop_sums()
        combine(jnp.maximum(blocks - 1, 0))

    pl.run_scoped(
        products,
        [pltpu.ACC(0)((CHUNK - DIRECT, BLOCK), f32)] * 2,
        [pltpu.ACC(0)((CHUNK, BLOCK), f32)] * 2,
        *[pltpu.ACC(1)((16, BLOCK), f32)] * 2,
        *[pltpu.ACC(1)((32, BLOCK), f32)] * 2,
    )

    def unpack(where, offset):
        shift = offset % 128
        base = pl.multiple_of(offset - shift, 128)
        x = sums[:, pl.ds(base, HALF + 128)]
        x = pltpu.roll(x, (HALF + 128) - shift, 1)
        for p in range(PAIRS):
            outs[p][where[p]] = fold(x[2 * p:2 * p + 2, 0:HALF])
        return offset + count[0, where[0]]

    owners(unpack)


def pair_scratch():
    return [
        pltpu.VMEM((8, ROOM), f32),
        pltpu.VMEM((8, ROOM), f32),
        pltpu.VMEM((256, BLOCK), bf16),
        pltpu.VMEM((2, 3, 8, BLOCK), f32),
        pltpu.VMEM((96, BLOCK), f32),
        pltpu.VMEM((8, 128), jnp.int32),
        pltpu.SMEM((8, 128), jnp.int32),
        pltpu.SemaphoreType.DMA,
    ]


def reduce_kernel(
    part0, part1, part2, start_ref, count_ref, out_ref,
    got_1, got_2, got_3, got_other, sum_1, sum_2, send_sem, recv_sem,
):
    part = (part0, part1, part2)
    barrier, greeted = greet()
    me, core = place()
    started = []

    def send(p, k, src, dst, target):
        c = pltpu.make_async_remote_copy(
            src_ref=src, dst_ref=dst, send_sem=send_sem.at[p, k],
            recv_sem=recv_sem.at[p, k], device_id=target, device_id_type=MESH,
        )
        c.start()
        started.append(c)
        return c

    pl.semaphore_wait(barrier, greeted)
    first = [[] for _ in range(PAIRS)]
    for p in range(PAIRS):
        axis = AXES[p][2]
        for d in (1, 2, 3):
            first[p].append(send(
                p, d - 1, part[p].at[(me[axis] + d) % 4], got_1[p].at[d - 1],
                along(me, core, axis, d),
            ))
    second = [[] for _ in range(PAIRS)]
    for p in range(PAIRS):
        axis = AXES[p][0]
        for c in first[p]:
            c.wait_recv()
        own = part[p][me[AXES[p][2]]]
        sum_1[p][...] = own + (got_1[p][0] + got_1[p][1] + got_1[p][2])
        for d in (1, 2, 3):
            line = pl.ds((me[axis] + d) % 4 * 4, 4)
            second[p].append(send(
                p, 2 + d, sum_1[p].at[line], got_2[p].at[d - 1], along(me, core, axis, d)
            ))
    last = [[] for _ in range(PAIRS)]
    for p in range(PAIRS):
        axis = AXES[p][1]
        for c in second[p]:
            c.wait_recv()
        own = sum_1[p][pl.ds(me[AXES[p][0]] * 4, 4)]
        sum_2[p][...] = own + (got_2[p][0] + got_2[p][1] + got_2[p][2])
        for d in (1, 2, 3):
            last[p].append(send(
                p, 5 + d, sum_2[p].at[(me[axis] + d) % 4, core], got_3[p].at[d - 1],
                along(me, core, axis, d),
            ))
        for d in range(4):
            last[p].append(send(
                p, 9 + d, sum_2[p].at[(me[axis] + d) % 4, 1 - core], got_other[p].at[d],
                along(me, 1 - core, axis, d),
            ))
    mine, others = [], []
    for p in range(PAIRS):
        for c in last[p]:
            c.wait_recv()
        own = sum_2[p][me[AXES[p][1]], core]
        mine.append(own + (got_3[p][0] + got_3[p][1] + got_3[p][2]))
        others.append(
            (got_other[p][0] + got_other[p][1]) + (got_other[p][2] + got_other[p][3])
        )
    mine, others = unfold(mine), unfold(others)
    halves = [jnp.where(core == 0, mine, others), jnp.where(core == 0, others, mine)]
    total = jnp.concatenate(
        [jnp.concatenate(halves, axis=1), jnp.zeros((2, SLOTS), f32)], axis=0
    )
    total = jnp.where(slot_of((8, SLOTS), 1) < count_ref[0], total, 0.0)
    total = reorder(total, True) * (1.0 / (STARS * OWNERS))
    start = start_ref[...]
    step = start[12:13]
    acc0, jerk0 = start[6:9], start[9:12]
    acc1, jerk1 = total[0:3], total[3:6]
    vel1 = start[3:6] + (acc0 + acc1) * step / 2.0 + (jerk0 - jerk1) * step * step / 12.0
    pos1 = start[0:3] + (start[3:6] + vel1) * step / 2.0 + (acc0 - acc1) * step * step / 12.0
    state = jnp.concatenate([pos1, vel1, acc1, jerk1], axis=0)
    live = lax.broadcasted_iota(jnp.int32, (12, SLOTS), 1) < count_ref[0]
    out_ref[...] = jnp.where(live, state, 0.0)
    for c in started:
        c.wait_send()


def shards(
    positions, velocities, old_acc, old_jerk, masses, elapsed, levels, active_index, active_count
):
    def lines(a):
        return a.reshape(STARS // 128, 128)

    def near(a):
        return pltpu.with_memory_space_constraint(a, pltpu.VMEM)

    def params(collective_id=None):
        extra = {} if collective_id is None else {
            "collective_id": collective_id, "has_side_effects": True
        }
        return pltpu.CompilerParams(vmem_limit_bytes=VMEM_LIMIT, **extra)

    *every, start, hq, hr, fw, fl, centre, wide = pl.pallas_call(
        gather_kernel,
        out_shape=[pltpu.VMEM(PLACES, f32)] * PAIRS + [
            pltpu.VMEM((16, SLOTS), f32),
            pltpu.VMEM((SOURCES, 128), bf16),
            pltpu.VMEM((SOURCES, 128), bf16),
            pltpu.VMEM((16, SOURCES), bf16),
            pltpu.VMEM((32, SOURCES), f8),
            pltpu.VMEM((8, 128), f32),
            pltpu.VMEM((3, SOURCES // CHUNK * DIRECT, 128), f32),
        ],
        in_specs=[vmem()] * 8 + [smem()],
        out_specs=[vmem()] * (PAIRS + 7),
        scratch_shapes=[
            pltpu.VMEM((16, STARS), f32),
            pltpu.VMEM((2, 8, STARS), f32),
            pltpu.VMEM((PAIRS, 4, 128), f32),
            pltpu.SemaphoreType.DMA((PAIRS, 14)),
            pltpu.SemaphoreType.DMA((PAIRS, 14)),
        ],
        compiler_params=params(0),
        name="predict_gather",
    )(
        *[
            pltpu.with_memory_space_constraint(a, pltpu.HBM)
            for a in (positions, velocities, old_acc, old_jerk, lines(masses), lines(elapsed),
                      lines(levels), active_index)
        ],
        active_count,
    )
    parts = pl.pallas_call(
        pair_kernel,
        out_shape=[pltpu.VMEM((OWNERS, 4, 128), f32)] * PAIRS,
        in_specs=[vmem()] * 9,
        out_specs=[vmem()] * PAIRS,
        scratch_shapes=pair_scratch(),
        compiler_params=params(),
        name="pair_sums",
    )(*[near(e.reshape(OWNERS, 4, 128)) for e in every], near(hq), near(hr), near(fw), near(fl), near(centre), near(wide))

    def buffers(*shape):
        return [pltpu.VMEM(shape + (4, 128), f32)] * PAIRS

    return pl.pallas_call(
        reduce_kernel,
        out_shape=jax.ShapeDtypeStruct((12, SLOTS), f32),
        in_specs=[vmem()] * (PAIRS + 1) + [smem()],
        out_specs=vmem(),
        scratch_shapes=[
            buffers(3, 16, 2),
            buffers(3, 4, 2),
            buffers(3),
            buffers(4),
            buffers(16, 2),
            buffers(4, 2),
            pltpu.SemaphoreType.DMA((PAIRS, 14)),
            pltpu.SemaphoreType.DMA((PAIRS, 14)),
        ],
        compiler_params=params(1),
        name="reduce_correct",
    )(*[near(p.reshape(PLACES)) for p in parts], near(start), active_count)


def solution(mesh):
    every = ("ia", "ja")
    in_specs = (
        P(None, every), P(None, every), P(None, every), P(None, every),
        P(every), P(every), P(every), P(every, None), P(every),
    )
    return jax.shard_map(
        shards, mesh=mesh, in_specs=in_specs, out_specs=P(None, every), check_vma=False
    )
```

```python
import jax
import jax.numpy as jnp
from jax import lax
from jax.experimental import pallas as pl
from jax.experimental.pallas import tpu as pltpu
from jax.sharding import PartitionSpec as P

MESH = pl.DeviceIdType.MESH
soften = 0.01
f32 = jnp.float32
bf16 = jnp.bfloat16
f8 = jnp.float8_e4m3fn

STARS = 1536
SLOTS = 512
SOURCES = 2 * STARS
HALF = SLOTS // 2
OWNERS = 128
BLOCK = 256
CHUNK = 256
TURN = 2
DIRECT = 32
ROOM = OWNERS * HALF + HALF + 128
VMEM_LIMIT = 24 * 2**20
PAIRS = 3
AXES = ("xyz", "yzx", "zxy")
PLACES = (4, 16, 2, 4, 128)
POS_SCALE = 2.0**-2
VEL_SCALE = 2.0**-8
W_SCALE = 2.0**6


def vmem():
    return pl.BlockSpec(memory_space=pltpu.VMEM)


def smem():
    return pl.BlockSpec(memory_space=pltpu.SMEM)


def split3(x):
    a = x.astype(bf16).astype(f32)
    rest = x - a
    b = rest.astype(bf16).astype(f32)
    return a, b, rest - b


def place():
    ia, ja = lax.axis_index("ia"), lax.axis_index("ja")
    return {"z": ia // 2, "x": (ia % 2) * 2 + (ja // 2) % 2, "y": ja // 4}, ja % 2


def device(at, core):
    return (at["z"] * 2 + at["x"] // 2, at["y"] * 4 + (at["x"] % 2) * 2 + core)


def along(me, core, axis, d):
    return device({**me, axis: (me[axis] + d) % 4}, core)


def greet():
    me, core = place()
    barrier = pltpu.get_barrier_semaphore()
    peers = [along(me, c, axis, d) for c in (core, 1 - core) for axis in "xyz" for d in (1, 2, 3)]
    for peer in [device(me, 1 - core)] + peers:
        pl.semaphore_signal(barrier, inc=1, device_id=peer, device_id_type=MESH)
    return barrier, 1 + len(peers)


def predict(d, step):
    tau_sq = 0.5 * step * step
    tau_cube = step * step * step / 6.0
    pos = d[0:3] + step * d[3:6] + tau_sq * d[6:9] + tau_cube * d[9:12]
    vel = d[3:6] + step * d[6:9] + tau_sq * d[9:12]
    return pos, vel


def flat(ref):
    return jnp.concatenate([ref[i:i + 1, :] for i in range(STARS // 128)], axis=1)


def fold(rows):
    return jnp.concatenate([rows[:, 128 * t:128 * (t + 1)] for t in range(2)], axis=0)


def unfold(blocks):
    return jnp.concatenate(
        [jnp.concatenate([b[2 * t:2 * t + 2] for b in blocks], axis=0) for t in range(2)], axis=1
    )


def slot_of(shape, axis):
    j = lax.broadcasted_iota(jnp.int32, shape, axis)
    return jnp.where(j < HALF, 2 * j, 2 * j - (SLOTS - 1))


def reordering(back):
    own = lax.broadcasted_iota(jnp.int32, (SLOTS, SLOTS), 1 if back else 0)
    return (own == slot_of((SLOTS, SLOTS), 0 if back else 1)).astype(f32).astype(bf16)


def reorder(rows, move):
    n = rows.shape[0]
    parts = jnp.concatenate(split3(rows), axis=0).astype(bf16)
    out = jnp.dot(parts, move, preferred_element_type=f32)
    return (out[0:n] + out[n:2 * n]) + out[2 * n:3 * n]


def gather_kernel(
    pos_ref, vel_ref, acc_ref, jerk_ref, mass_ref, elapsed_ref, levels_ref, index_ref, count_ref,
    all0, all1, all2, start_ref, hq_ref, hr_ref, fw_ref, f8_ref, centre_ref, wide_ref,
    state, src_ref, other, send_sem, recv_sem,
):
    every = (all0, all1, all2)
    barrier, greeted = greet()
    me, core = place()
    started = []

    def send(p, k, src, dst, target):
        c = pltpu.make_async_remote_copy(
            src_ref=src, dst_ref=dst, send_sem=send_sem.at[p, k],
            recv_sem=recv_sem.at[p, k], device_id=target, device_id_type=MESH,
        )
        c.start()
        started.append(c)
        return c

    state[...] = jnp.zeros_like(state)
    state[0:3] = pos_ref[...]
    state[3:6] = vel_ref[...]
    state[6:9] = acc_ref[...]
    state[9:12] = jerk_ref[...]
    levels = flat(levels_ref)
    step = jnp.where(
        levels == 0, 0.5, jnp.where(levels == 1, 0.25, jnp.where(levels == 2, 0.125, 0.0625))
    ).astype(f32)
    state[12:13] = step

    pick = (lax.broadcasted_iota(jnp.int32, (STARS, SLOTS), 0) == index_ref[...]).astype(f32)
    pick = pick.astype(bf16)
    parts = jnp.concatenate(split3(state[...]), axis=0).astype(bf16)
    rows = jnp.dot(parts, pick, preferred_element_type=f32)
    start = (rows[0:16] + rows[16:32]) + rows[32:48]
    start_ref[...] = start
    target = jnp.concatenate(predict(start, start[12:13]), axis=0)
    live = lax.broadcasted_iota(jnp.int32, (8, SLOTS), 1) < count_ref[0]
    target = reorder(jnp.concatenate([target, jnp.zeros((2, SLOTS), f32)], axis=0), reordering(False))
    marks = slot_of((8, SLOTS), 1) < count_ref[0]
    pairs = (jnp.where(marks[0:2], target[0:2], 1e30), target[2:4], target[4:6])
    for p in range(PAIRS):
        one, two, three = (me[axis] for axis in AXES[p])
        even, odd = fold(pairs[p][:, 0:HALF]), fold(pairs[p][:, HALF:])
        every[p][three, one * 4 + two, core] = jnp.where(core == 0, even, odd)
        other[p] = jnp.where(core == 0, odd, even)

    pl.semaphore_wait(barrier, greeted)

    flight = [[] for _ in range(PAIRS)]

    def begin(phase):
        for p in range(PAIRS):
            for c in flight[p]:
                c.wait_recv()
            one, two, three = (me[axis] for axis in AXES[p])
            block = every[p].at[three]
            if phase == 0:
                block = block.at[one * 4 + two, core]
            elif phase == 1:
                block = block.at[pl.ds(one * 4, 4)]
            axis = AXES[p][(1, 0, 2)[phase]]
            flight[p] = [
                send(p, 3 * phase + d - 1, block, block, along(me, core, axis, d))
                for d in (2, 1, 3)
            ]
            if phase == 0:
                flight[p] += [
                    send(p, 9 + d, other.at[p], block, along(me, 1 - core, axis, d))
                    for d in range(4)
                ]

    def finish():
        for p in range(PAIRS):
            for c in flight[p]:
                c.wait_recv()

    begin(0)
    chosen = lax.dot_general(
        live.astype(f32).astype(bf16), pick, (((1,), (1,)), ((), ())),
        preferred_element_type=f32,
    )[0:1]
    interval = jnp.where(chosen > 0.5, step, flat(elapsed_ref))
    src = jnp.concatenate(predict(state[...], interval), axis=0)
    mass = flat(mass_ref)
    src_ref[core] = jnp.concatenate([src, mass, jnp.zeros_like(mass)], axis=0)
    share = send(0, 13, src_ref.at[core], src_ref.at[core], device(me, 1 - core))
    begin(1)
    share.wait_recv()

    src = jnp.concatenate([src_ref[0], src_ref[1]], axis=1)
    mass = src[6:7]
    src = src[0:6]
    centre = jnp.sum(src, axis=1, keepdims=True) * (1.0 / SOURCES)
    centre = jnp.floor(centre * 64.0 + 0.5) * (1.0 / 64.0)
    src = src - centre
    centre = jnp.concatenate([centre, jnp.zeros((2, 1), f32)], axis=0)
    centre_ref[...] = jnp.broadcast_to(centre, (8, 128))
    zero = jnp.zeros((1, SOURCES), f32)
    weights = jnp.concatenate([src, zero + 1.0, zero], axis=0) * mass
    pos, vel = src[0:3] * POS_SCALE, src[3:6] * VEL_SCALE
    row = lax.broadcasted_iota(jnp.int32, (8, 1), 0)

    def factors(own, square, unit):
        a, b, c = split3(jnp.concatenate([own, zero, zero], axis=0))
        a = a + (row == unit).astype(f32)
        s = jnp.concatenate(split3(square) + (zero,) * 5, axis=0)
        fill = jnp.zeros((72, SOURCES), f32)
        return jnp.concatenate([a, b, a, b, c, a, s, fill], axis=0).T.astype(bf16)

    square = pos[0:1] * pos[0:1] + pos[1:2] * pos[1:2] + pos[2:3] * pos[2:3]
    hq_ref[...] = factors(jnp.concatenate([pos * -2.0, zero, zero, zero], axis=0), square, 6)
    begin(2)
    product = pos[0:1] * vel[0:1] + pos[1:2] * vel[1:2] + pos[2:3] * vel[2:3]
    hr_ref[...] = factors(jnp.concatenate([-vel, -pos], axis=0), product, 7)
    fill = jnp.zeros((8, SOURCES), f32)
    fw_ref[...] = jnp.concatenate(split3(weights)[0:2], axis=0).astype(bf16)
    high = weights.astype(f8).astype(f32)
    f8_ref[...] = jnp.concatenate([high, weights - high, fill, fill], axis=0).astype(f8)

    columns = jnp.concatenate([pos, jnp.zeros((5, SOURCES), f32)], axis=0)
    for c in range(SOURCES // CHUNK):
        some = columns[:, c * CHUNK:c * CHUNK + 128].T
        for axis in range(3):
            wide_ref[axis, c * DIRECT:(c + 1) * DIRECT] = jnp.broadcast_to(
                some[0:DIRECT, axis:axis + 1], (DIRECT, 128)
            )
    finish()
    for c in started:
        c.wait_send()


def pair_kernel(
    all0, all1, all2, hq, hr, fw, fl, centre_ref, wide_ref,
    out0, out1, out2,
    comp, sums, factor, near_ref, raw, counts, count, sem,
):
    outs = (out0, out1, out2)
    marked = jnp.where(all0[...] < 1e29, 0.5, 0.0)
    counted = jnp.sum(jnp.sum(marked, axis=1), axis=1, keepdims=True)
    counted = jnp.broadcast_to(counted, (OWNERS, 128)).T[0:8]
    counts[...] = counted.astype(jnp.int32)
    copy = pltpu.make_async_copy(counts, count, sem)
    copy.start()
    copy.wait()

    lane = lax.broadcasted_iota(jnp.int32, (8, 128), 1)
    blank = jnp.zeros((2, HALF), f32)

    def owners(step):
        def some(g, offset):
            core, z = g % 2, g // 2
            for x in range(4):
                for y in range(4):
                    at = {"x": x, "y": y, "z": z}
                    where = [
                        (at[three] * 16 + at[one] * 4 + at[two]) * 2 + core
                        for one, two, three in AXES
                    ]
                    offset = step(where, offset)
            return offset

        return lax.fori_loop(0, 8, some, jnp.int32(0))

    def pack(where, offset):
        shift = offset % 128
        base = pl.multiple_of(offset - shift, 128)
        x = unfold([ref[k] for ref, k in zip((all0, all1, all2), where)])
        x = jnp.concatenate([x, blank], axis=0)
        x = jnp.concatenate([x, jnp.zeros((8, 128), f32)], axis=1)
        x = pltpu.roll(x, shift, 1)
        first = pl.ds(base, 128)
        comp[:, first] = jnp.where(lane < shift, comp[:, first], x[:, 0:128])
        comp[:, pl.ds(base + 128, HALF)] = x[:, 128:]
        return offset + count[0, where[0]]

    total = owners(pack)
    blocks = (total + BLOCK - 1) // BLOCK
    centre = centre_ref[:, 0:1]
    row = lax.broadcasted_iota(jnp.int32, (8, 1), 0)
    scale = jnp.where(row < 3, POS_SCALE, VEL_SCALE)

    def columns(i):
        return pl.ds(pl.multiple_of(i * BLOCK, BLOCK), BLOCK)

    def make_factor(i, k):
        t = (comp[:, columns(i)] - centre) * scale
        for axis in range(3):
            near_ref[k, axis] = jnp.broadcast_to(t[axis:axis + 1], (8, BLOCK))
        square = t[0:1] * t[0:1] + t[1:2] * t[1:2] + t[2:3] * t[2:3] + soften * POS_SCALE**2
        product = t[0:1] * t[3:4] + t[1:2] * t[4:5] + t[2:3] * t[5:6]
        a, b, c = split3(jnp.concatenate([t[0:6], square, product], axis=0))
        ones = jnp.ones((8, BLOCK), f32)
        fill = jnp.zeros((200, BLOCK), f32)
        factor[...] = jnp.concatenate([a, a, b, b, a, c, ones, fill], axis=0).astype(bf16)

    def combine(i):
        sw = raw[0:8] + (raw[8:16] + (raw[32:40] + raw[40:48]))
        sb = raw[16:24] + (raw[24:32] + (raw[64:72] + raw[72:80]))
        t = comp[:, columns(i)] - centre
        rw = (sw - t * sw[6:7]) * (1.0 / W_SCALE)
        rb = pltpu.roll(sb - t * sb[6:7], 3, 0)
        sums[:, columns(i)] = rw - jnp.where((row >= 3) & (row < 6), 3.0 * rb, 0.0)

    def products(acc_q, acc_r, acc_w, acc_b, acc_lw, acc_lb):
        def stage_one(c, buffer, load):
            part = slice(c * CHUNK, (c + 1) * CHUNK)
            blank = jnp.zeros((CHUNK, 128), bf16)
            pltpu.matmul_acc_lhs(
                acc_r[buffer], jnp.concatenate([hr[part], blank], axis=1), load_staged_rhs=load
            )
            part = slice(c * CHUNK + DIRECT, (c + 1) * CHUNK)
            pltpu.matmul_acc_lhs(
                acc_q[buffer], jnp.concatenate([hq[part], blank[DIRECT:]], axis=1)
            )

        def direct(c, k):
            total = None
            for axis in range(3):
                wide = wide_ref[axis, c * DIRECT:(c + 1) * DIRECT]
                wide = jnp.concatenate([wide] * (BLOCK // 128), axis=1)
                gap = wide - jnp.concatenate([near_ref[k, axis]] * (DIRECT // 8), axis=0)
                total = gap * gap if total is None else total + gap * gap
            return total + soften * POS_SCALE**2

        def stage_factor(i, k):
            make_factor(i, k)
            pltpu.matmul_push_rhs(factor[...], 0, 0)

        def pop_sums():
            raw[0:16] = pltpu.matmul_pop(acc_w)
            raw[16:32] = pltpu.matmul_pop(acc_b)
            raw[32:64] = pltpu.matmul_pop(acc_lw)
            raw[64:96] = pltpu.matmul_pop(acc_lb)

        chunks = SOURCES // CHUNK

        def block(i, k):
            for c in range(chunks):
                if c == chunks - 1:
                    stage_factor(i + 1, 1 - k)
                    stage_one(0, 0, 0)
                else:
                    stage_one(c + 1, (c + 1) % 2, None)
                q = jnp.concatenate([direct(c, k), pltpu.matmul_pop(acc_q[c % 2])], axis=0)
                rv = pltpu.matmul_pop(acc_r[c % 2])
                inv = lax.rsqrt(q)
                inv2 = inv * inv
                w = inv2 * inv
                b = w * inv2 * rv
                w_high = w.astype(bf16)
                b_high = b.astype(bf16)
                w_low = (w - w_high.astype(f32)).astype(f8)
                b_low = (b - b_high.astype(f32)).astype(f8)
                if c == 0:
                    pop_sums()
                part = slice(c * CHUNK, (c + 1) * CHUNK)
                pltpu.matmul_push_rhs(w_high, 0, 1)
                pltpu.matmul_acc_lhs(acc_w, fw[:, part], load_staged_rhs=0)
                pltpu.matmul_push_rhs(b_high, 1, 1)
                pltpu.matmul_acc_lhs(acc_b, fw[:, part], load_staged_rhs=1)
                pltpu.matmul_push_rhs(w_low, 0, 1)
                pltpu.matmul_acc_lhs(acc_lw, fl[:, part], load_staged_rhs=0)
                pltpu.matmul_push_rhs(b_low, 1, 1)
                pltpu.matmul_acc_lhs(acc_lb, fl[:, part], load_staged_rhs=1)
                if c == 0:
                    combine(jnp.maximum(i - 1, 0))

        def several(j, carry):
            for k in range(TURN):
                block(j * TURN + k, k)
            return carry

        pop_sums()
        for k in range(2):
            pltpu.matmul_pop(acc_q[k])
            pltpu.matmul_pop(acc_r[k])
        stage_factor(0, 0)
        stage_one(0, 0, 0)
        lax.fori_loop(0, blocks // TURN, several, 0)

        def single(i, carry):
            block(i, 0)
            return carry

        lax.fori_loop(blocks // TURN * TURN, blocks, single, 0)
        pltpu.matmul_pop(acc_q[0])
        pltpu.matmul_pop(acc_r[0])
        pop_sums()
        combine(jnp.maximum(blocks - 1, 0))

    pl.run_scoped(
        products,
        [pltpu.ACC(0)((CHUNK - DIRECT, BLOCK), f32)] * 2,
        [pltpu.ACC(0)((CHUNK, BLOCK), f32)] * 2,
        *[pltpu.ACC(1)((16, BLOCK), f32)] * 2,
        *[pltpu.ACC(1)((32, BLOCK), f32)] * 2,
    )

    def unpack(where, offset):
        shift = offset % 128
        base = pl.multiple_of(offset - shift, 128)
        x = sums[:, pl.ds(base, HALF + 128)]
        x = pltpu.roll(x, (HALF + 128) - shift, 1)
        for p in range(PAIRS):
            outs[p][where[p]] = fold(x[2 * p:2 * p + 2, 0:HALF])
        return offset + count[0, where[0]]

    owners(unpack)


def pair_scratch():
    return [
        pltpu.VMEM((8, ROOM), f32),
        pltpu.VMEM((8, ROOM), f32),
        pltpu.VMEM((256, BLOCK), bf16),
        pltpu.VMEM((2, 3, 8, BLOCK), f32),
        pltpu.VMEM((96, BLOCK), f32),
        pltpu.VMEM((8, 128), jnp.int32),
        pltpu.SMEM((8, 128), jnp.int32),
        pltpu.SemaphoreType.DMA,
    ]


def reduce_kernel(
    part0, part1, part2, start_ref, count_ref, out_ref,
    got_1, got_2, got_3, got_other, sum_1, sum_2, move, send_sem, recv_sem,
):
    part = (part0, part1, part2)
    barrier, greeted = greet()
    me, core = place()
    started = []

    def send(p, k, src, dst, target):
        c = pltpu.make_async_remote_copy(
            src_ref=src, dst_ref=dst, send_sem=send_sem.at[p, k],
            recv_sem=recv_sem.at[p, k], device_id=target, device_id_type=MESH,
        )
        c.start()
        started.append(c)
        return c

    pl.semaphore_wait(barrier, greeted)
    first = [[] for _ in range(PAIRS)]
    for p in range(PAIRS):
        axis = AXES[p][2]
        for d in (1, 2, 3):
            first[p].append(send(
                p, d - 1, part[p].at[(me[axis] + d) % 4], got_1[p].at[d - 1],
                along(me, core, axis, d),
            ))
    move[...] = reordering(True)
    second = [[] for _ in range(PAIRS)]
    for p in range(PAIRS):
        axis = AXES[p][0]
        for c in first[p]:
            c.wait_recv()
        own = part[p][me[AXES[p][2]]]
        sum_1[p][...] = own + (got_1[p][0] + got_1[p][1] + got_1[p][2])
        for d in (1, 2, 3):
            line = pl.ds((me[axis] + d) % 4 * 4, 4)
            second[p].append(send(
                p, 2 + d, sum_1[p].at[line], got_2[p].at[d - 1], along(me, core, axis, d)
            ))
    last = [[] for _ in range(PAIRS)]
    for p in range(PAIRS):
        axis = AXES[p][1]
        for c in second[p]:
            c.wait_recv()
        own = sum_1[p][pl.ds(me[AXES[p][0]] * 4, 4)]
        sum_2[p][...] = own + (got_2[p][0] + got_2[p][1] + got_2[p][2])
        for d in (1, 2, 3):
            last[p].append(send(
                p, 5 + d, sum_2[p].at[(me[axis] + d) % 4, core], got_3[p].at[d - 1],
                along(me, core, axis, d),
            ))
        for d in range(4):
            last[p].append(send(
                p, 9 + d, sum_2[p].at[(me[axis] + d) % 4, 1 - core], got_other[p].at[d],
                along(me, 1 - core, axis, d),
            ))
    mine, others = [], []
    for p in range(PAIRS):
        for c in last[p]:
            c.wait_recv()
        own = sum_2[p][me[AXES[p][1]], core]
        mine.append(own + (got_3[p][0] + got_3[p][1] + got_3[p][2]))
        others.append(
            (got_other[p][0] + got_other[p][1]) + (got_other[p][2] + got_other[p][3])
        )
    mine, others = unfold(mine), unfold(others)
    halves = [jnp.where(core == 0, mine, others), jnp.where(core == 0, others, mine)]
    total = jnp.concatenate(
        [jnp.concatenate(halves, axis=1), jnp.zeros((2, SLOTS), f32)], axis=0
    )
    total = jnp.where(slot_of((8, SLOTS), 1) < count_ref[0], total, 0.0)
    total = reorder(total, move[...]) * (1.0 / (STARS * OWNERS))
    start = start_ref[...]
    step = start[12:13]
    acc0, jerk0 = start[6:9], start[9:12]
    acc1, jerk1 = total[0:3], total[3:6]
    vel1 = start[3:6] + (acc0 + acc1) * step / 2.0 + (jerk0 - jerk1) * step * step / 12.0
    pos1 = start[0:3] + (start[3:6] + vel1) * step / 2.0 + (acc0 - acc1) * step * step / 12.0
    state = jnp.concatenate([pos1, vel1, acc1, jerk1], axis=0)
    live = lax.broadcasted_iota(jnp.int32, (12, SLOTS), 1) < count_ref[0]
    out_ref[...] = jnp.where(live, state, 0.0)
    for c in started:
        c.wait_send()


def shards(
    positions, velocities, old_acc, old_jerk, masses, elapsed, levels, active_index, active_count
):
    def lines(a):
        return a.reshape(STARS // 128, 128)

    def near(a):
        return pltpu.with_memory_space_constraint(a, pltpu.VMEM)

    def params(collective_id=None):
        extra = {} if collective_id is None else {
            "collective_id": collective_id, "has_side_effects": True
        }
        return pltpu.CompilerParams(vmem_limit_bytes=VMEM_LIMIT, **extra)

    *every, start, hq, hr, fw, fl, centre, wide = pl.pallas_call(
        gather_kernel,
        out_shape=[pltpu.VMEM(PLACES, f32)] * PAIRS + [
            pltpu.VMEM((16, SLOTS), f32),
            pltpu.VMEM((SOURCES, 128), bf16),
            pltpu.VMEM((SOURCES, 128), bf16),
            pltpu.VMEM((16, SOURCES), bf16),
            pltpu.VMEM((32, SOURCES), f8),
            pltpu.VMEM((8, 128), f32),
            pltpu.VMEM((3, SOURCES // CHUNK * DIRECT, 128), f32),
        ],
        in_specs=[vmem()] * 8 + [smem()],
        out_specs=[vmem()] * (PAIRS + 7),
        scratch_shapes=[
            pltpu.VMEM((16, STARS), f32),
            pltpu.VMEM((2, 8, STARS), f32),
            pltpu.VMEM((PAIRS, 4, 128), f32),
            pltpu.SemaphoreType.DMA((PAIRS, 14)),
            pltpu.SemaphoreType.DMA((PAIRS, 14)),
        ],
        compiler_params=params(0),
        name="predict_gather",
    )(
        *[
            pltpu.with_memory_space_constraint(a, pltpu.HBM)
            for a in (positions, velocities, old_acc, old_jerk, lines(masses), lines(elapsed),
                      lines(levels), active_index)
        ],
        active_count,
    )
    parts = pl.pallas_call(
        pair_kernel,
        out_shape=[pltpu.VMEM((OWNERS, 4, 128), f32)] * PAIRS,
        in_specs=[vmem()] * 9,
        out_specs=[vmem()] * PAIRS,
        scratch_shapes=pair_scratch(),
        compiler_params=params(),
        name="pair_sums",
    )(*[near(e.reshape(OWNERS, 4, 128)) for e in every], near(hq), near(hr), near(fw), near(fl), near(centre), near(wide))

    def buffers(*shape):
        return [pltpu.VMEM(shape + (4, 128), f32)] * PAIRS

    return pl.pallas_call(
        reduce_kernel,
        out_shape=jax.ShapeDtypeStruct((12, SLOTS), f32),
        in_specs=[vmem()] * (PAIRS + 1) + [smem()],
        out_specs=vmem(),
        scratch_shapes=[
            buffers(3, 16, 2),
            buffers(3, 4, 2),
            buffers(3),
            buffers(4),
            buffers(16, 2),
            buffers(4, 2),
            pltpu.VMEM((SLOTS, SLOTS), bf16),
            pltpu.SemaphoreType.DMA((PAIRS, 14)),
            pltpu.SemaphoreType.DMA((PAIRS, 14)),
        ],
        compiler_params=params(1),
        name="reduce_correct",
    )(*[near(p.reshape(PLACES)) for p in parts], near(start), active_count)


def solution(mesh):
    every = ("ia", "ja")
    in_specs = (
        P(None, every), P(None, every), P(None, every), P(None, every),
        P(every), P(every), P(every), P(every, None), P(every),
    )
    return jax.shard_map(
        shards, mesh=mesh, in_specs=in_specs, out_specs=P(None, every), check_vma=False
    )
```
